512 devices in a mesh: prompt: 16 (over x, z_hi), resp: 32 (over z_lo, y, core).
Axes of the slice: x: 4, y: 8, z: 8 (z_hi: 4, z_lo: 2; z = z_hi * 2 + z_lo), core: 2. Of those that a mesh axis runs over, the one named last changes fastest.
Arguments:
- query: bfloat16 [512, 256, 2048], P(('prompt', 'resp')), may hold values from -6 to 6
- resp_keys: bfloat16 [512, 256, 512], P(('prompt', 'resp')), may hold values from -6 to 6
- resp_values: bfloat16 [512, 256, 512], P(('prompt', 'resp')), may hold values from -6 to 6
- prompt_keys: bfloat16 [8, 128, 512], P(None, 'prompt'), may hold values from -6 to 6
- prompt_values: bfloat16 [8, 128, 512], P(None, 'prompt'), may hold values from -6 to 6
- out_grad: bfloat16 [512, 256, 2048], P(('prompt', 'resp')), may hold values from -6 to 6
- group: int32 [512], replicated, may hold values from 0 to 7
- lengths: int32 [512], P(('prompt', 'resp')), may hold values from 1 to 256, 81920 in all
Outputs:
- query_grad: bfloat16 [512, 256, 2048], P(('prompt', 'resp'))
- resp_key_grad: bfloat16 [512, 256, 512], P(('prompt', 'resp'))
- resp_value_grad: bfloat16 [512, 256, 512], P(('prompt', 'resp'))
- prompt_key_grad: float32 [8, 128, 512], P(None, 'prompt')
- prompt_value_grad: float32 [8, 128, 512], P(None, 'prompt')
The draws below stay inside these ranges and needn't reach their ends.
Inputs may be any that keep to these rules, and one draw needn't show every extreme that they name: `group`: response r stands on device r of prompt+resp, in the mesh's order. `lengths`: a response's live tokens come first; some response fills all 256 slots.
All inputs are finite; a program needn't handle non-finite values. No bound on the sum of `lengths` on one device may be relied on, other than what follows from the above.
Results may differ from the reference program's by a relative error of at most 0.0097.
Values may be sent and summed in bfloat16 or wider, within the bound.
No kernel may reach another device: no remote copies, remote signals or barrier semaphores. Data moves between devices by JAX's collectives and lax.ppermute only.
A program may use at most 64 MiB of HBM per device.

```python
import math
import jax
import jax.numpy as jnp
import numpy as np
from jax import lax

QH = 16
KVH = 4
HD = 128
PROMPTS = 8
RLEN = 256
QW = 2048
KVW = 512
PLEN = 128
RESPONSES = 512


def draw_query(key, part):
    key = jax.random.fold_in(key, 11)
    shape_full = (RESPONSES, RLEN, QH, HD)
    drawn = jnp.clip(jax.random.normal(key, shape_full, jnp.float32), -6.0, 6.0)
    return drawn.reshape(RESPONSES, RLEN, QH * HD).astype(jnp.bfloat16)


def draw_prompt_keys(key, part):
    key = jax.random.fold_in(key, 12)
    shape_full = (PROMPTS, PLEN, KVH, HD)
    drawn = jnp.clip(jax.random.normal(key, shape_full, jnp.float32), -6.0, 6.0)
    return drawn.reshape(PROMPTS, PLEN, KVH * HD).astype(jnp.bfloat16)


def with_ends(values, rng, least, largest):
    longest = values.shape.index(max(values.shape))
    spots = []
    for shift in (0, 1):
        where = [jax.random.randint(jax.random.fold_in(rng, axis), (), 0, length) for axis, length in enumerate(values.shape)]
        where[longest] = (where[longest] + shift) % values.shape[longest]
        spots.append(tuple(where))
    return values.at[spots[0]].set(least).at[spots[1]].set(largest)


def shard_levels(key, extent, cuts, least, high):
    def one(position, shards_of):
        heights = jax.random.uniform(jax.random.fold_in(jax.random.fold_in(key, 6), position), (shards_of,), jnp.float32, least / len(cuts), high / len(cuts))
        return jnp.repeat(jnp.exp(heights), extent[position] // shards_of).reshape((-1,) + (1,) * (len(extent) - position - 1))

    factor_of = one(*cuts[0])
    for cut in cuts[1:]:
        factor_of = factor_of * one(*cut)
    return factor_of


def profile(number_of, total, bound, slope):
    weights = [(1 << 20) // math.isqrt(standing ** slope) + 1 for standing in range(2, number_of + 1)]
    surplus, counts = total - bound - (number_of - 1), [1] * (number_of - 1)
    while surplus > 0:
        movable = [i for i in range(number_of - 1) if counts[i] < bound]
        pool, budget = sum([weights[i] for i in movable]), surplus
        for i in movable:
            extra = min(bound - counts[i], max(1, budget * weights[i] // pool), surplus)
            counts[i] = counts[i] + extra
            surplus = surplus - extra
    return np.array([bound] + counts)


def ragged_sizes(own_key, number_of, total, bound, skew):
    if number_of == 2:
        one = jax.random.randint(own_key, (), max(1, total - bound), min(bound, total - 1) + 1)
        return jnp.stack([one, total - one])
    tallies = jnp.asarray(profile(number_of, total, bound, skew), jnp.int32)
    twos = (number_of - 1) // 2
    donor, taker = tallies[1:1 + 2 * twos:2], tallies[2:2 + 2 * twos:2]
    margin = jnp.minimum(donor - 1, bound - taker)
    shifted = jax.random.randint(jax.random.fold_in(own_key, 1), (twos,), 0, 1 << 20) % (margin + 1)
    tallies = tallies.at[1:1 + 2 * twos:2].set(donor - shifted).at[2:2 + 2 * twos:2].set(taker + shifted)
    return tallies[jax.random.permutation(jax.random.fold_in(own_key, 2), number_of)]


def scatter_about(stream_key, shape, scale, bound, pieces=(), kind=jnp.bfloat16):
    gain = shard_levels(stream_key, shape, pieces, -0.22, 0.18) if pieces else 1.0
    entries = jax.random.normal(stream_key, shape, jnp.float32) * scale * gain
    return jnp.minimum(jnp.maximum(entries, -bound), bound).astype(kind)


def setup_inputs(seed: int = 0) -> dict:
    key_list = jax.random.split(jax.random.key(seed), 9)
    return {
        "query": draw_query(jax.random.fold_in(key_list[8], 71), 0),
        "resp_keys": scatter_about(key_list[1], (RESPONSES, RLEN, KVW), 1.0, 6.0, ((0, 512),)),
        "resp_values": scatter_about(key_list[2], (RESPONSES, RLEN, KVW), 1.0, 6.0, ((0, 512),)),
        "prompt_keys": draw_prompt_keys(jax.random.fold_in(key_list[8], 71), 0),
        "prompt_values": scatter_about(key_list[4], (PROMPTS, PLEN, KVW), 1.0, 6.0, ((1, 16),)),
        "out_grad": scatter_about(key_list[5], (RESPONSES, RLEN, QW), 1.0, 6.0, ((0, 512),)),
        "group": with_ends(jax.random.randint(key_list[6], (RESPONSES,), 0, PROMPTS), jax.random.fold_in(key_list[6], 1), 0, PROMPTS - 1).astype(jnp.int32),
        "lengths": ragged_sizes(key_list[7], RESPONSES, RESPONSES * RLEN * 5 // 8, RLEN, 2).astype(jnp.int32),
    }


masked_score = -1e+30

def one_response(query_rows, own_keys, own_values, grad_rows, length, front_keys, front_values):
    all_keys = jnp.concatenate([front_keys, own_keys], 0)
    all_values = jnp.concatenate([front_values, own_values], 0)
    total_len = all_keys.shape[0]
    score_scale = 1.0 / math.sqrt(HD)
    row_ids = jnp.arange(RLEN)[:, None]
    col_ids = jnp.arange(total_len)[None, :]
    allowed = (col_ids < PLEN) | (col_ids - PLEN <= row_ids)
    live_rows = (jnp.arange(RLEN) < length)[:, None]
    grad_rows = jnp.where(live_rows, grad_rows, jnp.zeros_like(grad_rows))
    group_size = QH // KVH
    query_four = query_rows.reshape(RLEN, KVH, group_size, HD).astype(jnp.float32)
    grad_four = grad_rows.reshape(RLEN, KVH, group_size, HD).astype(jnp.float32)
    query_parts = []
    key_parts = []
    value_parts = []
    for kv_head in range(KVH):
        head_keys = all_keys[:, kv_head * HD:(kv_head + 1) * HD].astype(jnp.float32)
        head_values = all_values[:, kv_head * HD:(kv_head + 1) * HD].astype(jnp.float32)
        head_query = query_four[:, kv_head]
        head_grad = grad_four[:, kv_head]
        scores = jnp.einsum('igd,jd->gij', head_query, head_keys) * score_scale
        scores = jnp.where(allowed[None], scores, masked_score)
        row_max = lax.optimization_barrier(jnp.max(scores, -1, keepdims=True))
        weights = jnp.where(allowed[None], jnp.exp(scores - row_max), 0.0)
        attn_prob = weights / lax.optimization_barrier(jnp.sum(weights, -1, keepdims=True))
        prob_low = lax.optimization_barrier(attn_prob.astype(jnp.bfloat16)).astype(jnp.float32)
        attn_out = jnp.einsum('gij,jd->igd', prob_low, head_values)
        delta = jnp.einsum('igd,igd->gi', head_grad, attn_out)
        dprob = jnp.einsum('igd,jd->gij', head_grad, head_values)
        dscore = attn_prob * (dprob - delta[:, :, None])
        dscore_low = lax.optimization_barrier(dscore.astype(jnp.bfloat16)).astype(jnp.float32)
        query_term = jnp.einsum('gij,jd->igd', dscore_low, head_keys) * score_scale
        key_term = jnp.einsum('gij,igd->jd', dscore_low, head_query) * score_scale
        value_term = jnp.einsum('gij,igd->jd', prob_low, head_grad)
        query_parts.append(query_term.reshape(RLEN, group_size * HD))
        key_parts.append(key_term)
        value_parts.append(value_term)
    query_grad = jnp.concatenate(query_parts, -1).astype(jnp.bfloat16)
    key_all = jnp.concatenate(key_parts, -1)
    value_all = jnp.concatenate(value_parts, -1)
    return (query_grad, key_all[PLEN:].astype(jnp.bfloat16), value_all[PLEN:].astype(jnp.bfloat16), key_all[:PLEN], value_all[:PLEN])

def reference(query, resp_keys, resp_values, prompt_keys, prompt_values, out_grad, group, lengths):

    def advance(totals, inputs_row):
        query_rows, own_keys, own_values, grad_rows, owner_id, length = inputs_row
        front_keys = lax.dynamic_index_in_dim(prompt_keys, owner_id, 0, keepdims=False)
        front_values = lax.dynamic_index_in_dim(prompt_values, owner_id, 0, keepdims=False)
        query_grad, key_grad, value_grad, prompt_key, prompt_value = one_response(query_rows, own_keys, own_values, grad_rows, length, front_keys, front_values)
        hit_mask = (jnp.arange(PROMPTS) == owner_id)[:, None, None]
        key_total = totals[0] + jnp.where(hit_mask, prompt_key[None], 0.0)
        value_total = totals[1] + jnp.where(hit_mask, prompt_value[None], 0.0)
        return ((key_total, value_total), (query_grad, key_grad, value_grad))
    zero_grads = jnp.zeros((PROMPTS, PLEN, KVW), jnp.float32)
    sums, stacked = lax.scan(advance, (zero_grads, zero_grads), (query, resp_keys, resp_values, out_grad, group, lengths))
    return (stacked[0], stacked[1], stacked[2], sums[0], sums[1])
```

```python
import functools
import math

import jax
import jax.numpy as jnp
from jax import lax
from jax.experimental import pallas as pl
from jax.experimental.pallas import tpu as pltpu
from jax.sharding import PartitionSpec as P

HD = 128
KVH = 4
GROUP = 4
HALF = 128
SCALE = 1.0 / math.sqrt(HD)
LOG2E = math.log2(math.e)
BF16 = jnp.bfloat16
F32 = jnp.float32


def nt_dot(a, b):
    return lax.dot_general(a, b, (((1,), (1,)), ((), ())), preferred_element_type=F32)


def nn_dot(a, b):
    return lax.dot_general(a, b, (((1,), (0,)), ((), ())), preferred_element_type=F32)


def pick_kernel(peers_ref, keys_ref, values_ref, out_ref):
    for p in range(out_ref.shape[0]):
        owner = peers_ref[p]
        both = jnp.concatenate(
            [keys_ref[owner].astype(F32), values_ref[owner].astype(F32)], axis=0
        )
        out_ref[p] = both.astype(BF16)


def pick(peers, keys, values):
    count, (_, rows, width) = peers.shape[0], keys.shape
    return pl.pallas_call(
        pick_kernel,
        out_shape=jax.ShapeDtypeStruct((count, 2 * rows, width), BF16),
        in_specs=[
            pl.BlockSpec(memory_space=pltpu.SMEM),
            pl.BlockSpec(memory_space=pltpu.VMEM),
            pl.BlockSpec(memory_space=pltpu.VMEM),
        ],
        out_specs=pl.BlockSpec(memory_space=pltpu.VMEM),
    )(peers, keys, values)


def attend_kernel(
    length_ref,
    query_ref,
    grad_ref,
    keys_ref,
    values_ref,
    front_ref,
    query_grad_ref,
    key_grad_ref,
    value_grad_ref,
    front_grad_ref,
):
    length = length_ref[0]
    rows = query_ref.shape[0]
    shards_n, both, _ = front_ref.shape
    own = both // 2
    front_len = shards_n * own
    front = front_ref[...].astype(F32)
    all_keys = jnp.concatenate(
        [front[:, :own].reshape(front_len, HD).astype(BF16), keys_ref[...]], axis=0
    )
    all_values = jnp.concatenate(
        [front[:, own:].reshape(front_len, HD).astype(BF16), values_ref[...]], axis=0
    )
    keys_across = jnp.transpose(all_keys)
    wide = GROUP * HALF
    key_ids = lax.broadcasted_iota(jnp.int32, (HALF, wide), 0)
    row_ids = lax.broadcasted_iota(jnp.int32, (HALF, wide), 1) % HALF
    allowed = key_ids <= row_ids
    live_ids = lax.broadcasted_iota(jnp.int32, (HALF, GROUP * HD), 0)
    key_total = None
    value_total = None
    for half in range(rows // HALF):
        span = slice(half * HALF, (half + 1) * HALF)
        reach = front_len + (half + 1) * HALF
        query = query_ref[span, :]
        grad = grad_ref[span, :]
        grad = jnp.where(live_ids + half * HALF < length, grad, jnp.zeros_like(grad))
        query = jnp.concatenate(
            [query[:, g * HD : (g + 1) * HD] for g in range(GROUP)], axis=0
        )
        grad = jnp.concatenate(
            [grad[:, g * HD : (g + 1) * HD] for g in range(GROUP)], axis=0
        )
        scores = nt_dot(all_keys[:reach], query)
        scores = jnp.concatenate(
            [
                scores[: reach - HALF],
                jnp.where(allowed, scores[reach - HALF :], -1e30),
            ],
            axis=0,
        )
        row_max = jnp.max(scores, axis=0, keepdims=True)
        weights = jnp.exp2((scores - row_max) * (SCALE * LOG2E))
        prob = weights * (1.0 / jnp.sum(weights, axis=0, keepdims=True))
        prob_low = prob.astype(BF16)
        dprob = nt_dot(all_values[:reach], grad)
        delta = jnp.sum(prob_low.astype(F32) * dprob, axis=0, keepdims=True)
        dscore = (prob * (dprob - delta)).astype(BF16)
        query_term = nn_dot(keys_across[:, :reach], dscore) * SCALE
        for g in range(GROUP):
            query_grad_ref[span, g * HD : (g + 1) * HD] = jnp.transpose(
                query_term[:, g * HALF : (g + 1) * HALF]
            ).astype(BF16)
        key_term = nn_dot(dscore, query) * SCALE
        value_term = nn_dot(prob_low, grad)
        if key_total is None:
            key_total, value_total = key_term, value_term
        else:
            done = key_total.shape[0]
            key_total = jnp.concatenate(
                [key_total + key_term[:done], key_term[done:]], axis=0
            )
            value_total = jnp.concatenate(
                [value_total + value_term[:done], value_term[done:]], axis=0
            )
    key_grad_ref[...] = key_total[front_len:].astype(BF16)
    value_grad_ref[...] = value_total[front_len:].astype(BF16)
    front_grad_ref[...] = jnp.concatenate(
        [
            key_total[:front_len].reshape(shards_n, own, HD),
            value_total[:front_len].reshape(shards_n, own, HD),
        ],
        axis=1,
    ).astype(BF16)


def attend(length, query, grad, keys, values, front):
    rows, query_width = query.shape
    key_width = keys.shape[1]
    shards_n, both, _ = front.shape
    wide = pl.BlockSpec((rows, GROUP * HD), lambda k: (0, k))
    narrow = pl.BlockSpec((rows, HD), lambda k: (0, k))
    front_spec = pl.BlockSpec((shards_n, both, HD), lambda k: (0, 0, k))
    return pl.pallas_call(
        attend_kernel,
        grid=(KVH,),
        out_shape=(
            jax.ShapeDtypeStruct((rows, query_width), BF16),
            jax.ShapeDtypeStruct((rows, key_width), BF16),
            jax.ShapeDtypeStruct((rows, key_width), BF16),
            jax.ShapeDtypeStruct(front.shape, BF16),
        ),
        in_specs=[
            pl.BlockSpec(memory_space=pltpu.SMEM),
            wide,
            wide,
            narrow,
            narrow,
            front_spec,
        ],
        out_specs=(wide, narrow, narrow, front_spec),
        compiler_params=pltpu.CompilerParams(vmem_limit_bytes=48 * 1024 * 1024),
    )(length, query, grad, keys, values, front)


def add_kernel(peers_ref, terms_ref, out_ref, total):
    total[...] = jnp.zeros_like(total)
    for p in range(terms_ref.shape[0]):
        owner = peers_ref[p]
        total[owner] = total[owner] + terms_ref[p].astype(F32)
    for owner in range(total.shape[0]):
        for k in range(KVH):
            out_ref[owner * KVH + k] = total[owner, :, k * HD : (k + 1) * HD].astype(BF16)


def add_by_prompt(peers, terms, num_prompts):
    _, both, width = terms.shape
    return pl.pallas_call(
        add_kernel,
        out_shape=jax.ShapeDtypeStruct((num_prompts * KVH, both, HD), BF16),
        in_specs=[
            pl.BlockSpec(memory_space=pltpu.SMEM),
            pl.BlockSpec(memory_space=pltpu.VMEM),
        ],
        out_specs=pl.BlockSpec(memory_space=pltpu.VMEM),
        scratch_shapes=[pltpu.VMEM((num_prompts, both, width), F32)],
    )(peers, terms)


def shards(query, resp_keys, resp_values, prompt_keys, prompt_values, out_grad, group, lengths):
    resp_count = lax.axis_size("resp")
    resp_index = lax.axis_index("resp")
    num_prompts, own, width = prompt_keys.shape
    peers = lax.dynamic_index_in_dim(
        group.reshape(-1, resp_count), resp_index, 1, keepdims=False
    )
    front = lax.all_to_all(pick(peers, prompt_keys, prompt_values), "prompt", 0, 0)
    query_grad, key_grad, value_grad, front_grad = attend(
        lengths, query[0], out_grad[0], resp_keys[0], resp_values[0], front
    )
    terms = lax.all_to_all(front_grad, "prompt", 0, 0)
    sums = add_by_prompt(peers, terms, num_prompts)
    parts = lax.all_to_all(sums, "resp", 0, 0)
    mine = jnp.sum(parts.astype(F32), 0).astype(BF16)
    spread = jnp.broadcast_to(mine[None], (resp_count,) + mine.shape)
    whole = lax.all_to_all(spread, "resp", 0, 0).astype(F32)
    whole = whole.reshape(num_prompts, KVH, 2, own, HD).transpose(2, 0, 3, 1, 4)
    whole = whole.reshape(2, num_prompts, own, width)
    return (query_grad[None], key_grad[None], value_grad[None], whole[0], whole[1])


def solution(mesh):
    return jax.shard_map(
        shards,
        mesh=mesh,
        in_specs=(
            P(("prompt", "resp"), None, None),
            P(("prompt", "resp"), None, None),
            P(("prompt", "resp"), None, None),
            P(None, "prompt", None),
            P(None, "prompt", None),
            P(("prompt", "resp"), None, None),
            P(),
            P(("prompt", "resp")),
        ),
        out_specs=(
            P(("prompt", "resp"), None, None),
            P(("prompt", "resp"), None, None),
            P(("prompt", "resp"), None, None),
            P(None, "prompt", None),
            P(None, "prompt", None),
        ),
        check_vma=False,
    )
```

```python
import functools
import math

import jax
import jax.numpy as jnp
from jax import lax
from jax.experimental import pallas as pl
from jax.experimental.pallas import tpu as pltpu
from jax.sharding import Mesh
from jax.sharding import PartitionSpec as P

HD = 128
KVH = 4
GROUP = 4
CORES = 2
HALF = 128
SCALE = 1.0 / math.sqrt(HD)
LOG2E = math.log2(math.e)
BF16 = jnp.bfloat16
F32 = jnp.float32
SMEM = pl.BlockSpec(memory_space=pltpu.SMEM)
VMEM = pl.BlockSpec(memory_space=pltpu.VMEM)


def nt_dot(a, b):
    return lax.dot_general(a, b, (((1,), (1,)), ((), ())), preferred_element_type=F32)


def nn_dot(a, b):
    return lax.dot_general(a, b, (((1,), (0,)), ((), ())), preferred_element_type=F32)


def exp_scaled(x):
    return jnp.exp2(x * (SCALE * LOG2E))


def stack_heads(block, half, k=0):
    span = slice(half * HALF, (half + 1) * HALF)
    return jnp.concatenate(
        [block[span, h * HD : (h + 1) * HD] for h in range(k * GROUP, (k + 1) * GROUP)],
        axis=0,
    )


def live_grad(grad_ref, length, half, k=0):
    grad = stack_heads(grad_ref, half, k)
    row_ids = lax.broadcasted_iota(jnp.int32, grad.shape, 0) % HALF
    return jnp.where(row_ids + half * HALF < length, grad, jnp.zeros_like(grad))


def causal(scores):
    reach, wide = scores.shape
    key_ids = lax.broadcasted_iota(jnp.int32, (HALF, wide), 0)
    row_ids = lax.broadcasted_iota(jnp.int32, (HALF, wide), 1) % HALF
    last = jnp.where(key_ids <= row_ids, scores[reach - HALF :], -1e30)
    if reach == HALF:
        return last
    return jnp.concatenate([scores[: reach - HALF], last], axis=0)


def front_parts(front_ref, k=0):
    shards_n, both, _ = front_ref.shape
    front = front_ref[:, :, k * HD : (k + 1) * HD].astype(F32)
    keys, values = front[:, : both // 2], front[:, both // 2 :]
    return (
        keys.reshape(shards_n * both // 2, HD).astype(BF16),
        values.reshape(shards_n * both // 2, HD).astype(BF16),
    )


def pick_kernel(group_ref, keys_ref, values_ref, out_ref):
    place_along = lax.axis_index("chip") * CORES + lax.axis_index("core")
    count = out_ref.shape[0]
    stride = group_ref.shape[0] // count
    for p in range(count):
        owner = group_ref[p * stride + place_along]
        both = jnp.concatenate(
            [keys_ref[owner].astype(F32), values_ref[owner].astype(F32)], axis=0
        )
        out_ref[p] = both.astype(BF16)


def pick(group, keys, values, count):
    _, rows, width = keys.shape
    return pl.pallas_call(
        pick_kernel,
        out_shape=jax.ShapeDtypeStruct((count, 2 * rows, width), BF16),
        in_specs=[SMEM, VMEM, VMEM],
        out_specs=VMEM,
        compiler_params=params(56),
    )(group, keys, values)


def own_kernel(length_ref, query_ref, grad_ref, keys_ref, values_ref, stats_ref):
    length = length_ref[0]
    for k in range(KVH):
        features = slice(k * HD, (k + 1) * HD)
        for half in range(query_ref.shape[0] // HALF):
            reach = (half + 1) * HALF
            query = stack_heads(query_ref, half, k)
            grad = live_grad(grad_ref, length, half, k)
            scores = causal(nt_dot(keys_ref[:reach, features], query))
            top = jnp.max(scores, axis=0, keepdims=True)
            weights = exp_scaled(scores - top)
            dprob = nt_dot(values_ref[:reach, features], grad)
            total = jnp.sum(weights, axis=0, keepdims=True)
            dot = jnp.sum(weights * dprob, axis=0, keepdims=True)
            fill = jnp.zeros((5, top.shape[1]), F32)
            stats_ref[k, half] = jnp.concatenate([top, total, dot, fill], axis=0)


def front_kernel(
    length_ref, query_ref, grad_ref, front_ref, stats_ref, front_grad_ref, full_ref
):
    length = length_ref[0]
    shards_n, _, both, _ = front_grad_ref.shape
    for k in range(KVH):
        keys, values = front_parts(front_ref, k)
        key_total, value_total = 0.0, 0.0
        for half in range(query_ref.shape[0] // HALF):
            query = stack_heads(query_ref, half, k)
            grad = live_grad(grad_ref, length, half, k)
            stats = stats_ref[k, half]
            own_top, own_total, own_dot = stats[0:1], stats[1:2], stats[2:3]
            scores = nt_dot(keys, query)
            top = jnp.maximum(jnp.max(scores, axis=0, keepdims=True), own_top)
            weights = exp_scaled(scores - top)
            rescale = exp_scaled(own_top - top)
            total = jnp.sum(weights, axis=0, keepdims=True) + own_total * rescale
            inverse = 1.0 / total
            prob = weights * inverse
            prob_low = prob.astype(BF16)
            dprob = nt_dot(values, grad)
            delta = jnp.sum(prob * dprob, axis=0, keepdims=True) + own_dot * (
                rescale * inverse
            )
            dscore = (prob * (dprob - delta)).astype(BF16)
            key_total = key_total + nn_dot(dscore, query)
            value_total = value_total + nn_dot(prob_low, grad)
            fill = jnp.zeros((5, top.shape[1]), F32)
            full_ref[k, half] = jnp.concatenate([top, inverse, delta, fill], axis=0)
        front_grad_ref[:, k] = jnp.concatenate(
            [
                (key_total * SCALE).reshape(shards_n, both // 2, HD),
                value_total.reshape(shards_n, both // 2, HD),
            ],
            axis=1,
        ).astype(BF16)


def rest_kernel(
    length_ref,
    query_ref,
    grad_ref,
    keys_ref,
    values_ref,
    front_ref,
    full_ref,
    query_grad_ref,
    key_grad_ref,
    value_grad_ref,
):
    length = length_ref[0]
    front_keys, front_values = front_parts(front_ref)
    front_len = front_keys.shape[0]
    all_keys = jnp.concatenate([front_keys, keys_ref[...]], axis=0)
    all_values = jnp.concatenate([front_values, values_ref[...]], axis=0)
    keys_across = jnp.transpose(all_keys)
    key_total, value_total = None, None
    for half in range(query_ref.shape[0] // HALF):
        reach = front_len + (half + 1) * HALF
        span = slice(half * HALF, (half + 1) * HALF)
        query = stack_heads(query_ref, half)
        grad = live_grad(grad_ref, length, half)
        full = full_ref[half]
        top, inverse, delta = full[0:1], full[1:2], full[2:3]
        scores = causal(nt_dot(all_keys[:reach], query))
        prob = exp_scaled(scores - top) * inverse
        dprob = nt_dot(all_values[:reach], grad)
        dscore = (prob * (dprob - delta)).astype(BF16)
        query_term = nn_dot(keys_across[:, :reach], dscore) * SCALE
        for g in range(GROUP):
            query_grad_ref[span, g * HD : (g + 1) * HD] = jnp.transpose(
                query_term[:, g * HALF : (g + 1) * HALF]
            ).astype(BF16)
        key_term = nn_dot(dscore[front_len:], query)
        value_term = nn_dot(prob[front_len:].astype(BF16), grad)
        if key_total is None:
            key_total, value_total = key_term, value_term
        else:
            done = key_total.shape[0]
            key_total = jnp.concatenate(
                [key_total + key_term[:done], key_term[done:]], axis=0
            )
            value_total = jnp.concatenate(
                [value_total + value_term[:done], value_term[done:]], axis=0
            )
    key_grad_ref[...] = (key_total * SCALE).astype(BF16)
    value_grad_ref[...] = value_total.astype(BF16)


def attention_specs(rows, shards_n, both):
    wide = pl.BlockSpec((rows, GROUP * HD), lambda k: (0, k))
    narrow = pl.BlockSpec((rows, HD), lambda k: (0, k))
    front = pl.BlockSpec((shards_n, both, HD), lambda k: (0, 0, k))
    stats = pl.BlockSpec(
        (None, rows // HALF, 8, GROUP * HALF), lambda k: (k, 0, 0, 0)
    )
    return wide, narrow, front, stats


def params(mib):
    return pltpu.CompilerParams(vmem_limit_bytes=mib * 1024 * 1024)


def cost(matmuls, keys):
    flops = 2 * KVH * GROUP * 256 * keys * HD * matmuls
    return pl.CostEstimate(
        flops=flops, bytes_accessed=3 << 20, transcendentals=KVH * GROUP * 256 * keys
    )


def own_stats(length, query, grad, keys, values):
    rows = query.shape[0]
    return pl.pallas_call(
        own_kernel,
        out_shape=jax.ShapeDtypeStruct((KVH, rows // HALF, 8, GROUP * HALF), F32),
        in_specs=[SMEM, VMEM, VMEM, VMEM, VMEM],
        out_specs=VMEM,
        compiler_params=params(16),
        cost_estimate=cost(2, 256),
    )(length, query, grad, keys, values)


def front_part(length, query, grad, front, own):
    shards_n, both, _ = front.shape
    return pl.pallas_call(
        front_kernel,
        out_shape=(
            jax.ShapeDtypeStruct((shards_n, KVH, both, HD), BF16),
            jax.ShapeDtypeStruct(own.shape, F32),
        ),
        in_specs=[SMEM, VMEM, VMEM, VMEM, VMEM],
        out_specs=(VMEM, VMEM),
        compiler_params=params(16),
        cost_estimate=cost(4, 128),
    )(length, query, grad, front, own)


def rest_part(length, query, grad, keys, values, front, full):
    shards_n, both, _ = front.shape
    wide, narrow, front_spec, stats = attention_specs(query.shape[0], shards_n, both)
    return pl.pallas_call(
        rest_kernel,
        grid=(KVH,),
        out_shape=(
            jax.ShapeDtypeStruct(query.shape, BF16),
            jax.ShapeDtypeStruct(keys.shape, BF16),
            jax.ShapeDtypeStruct(values.shape, BF16),
        ),
        in_specs=[SMEM, wide, wide, narrow, narrow, front_spec, stats],
        out_specs=(wide, narrow, narrow),
        compiler_params=params(24),
        cost_estimate=cost(5, 384),
    )(length, query, grad, keys, values, front, full)


def add_kernel(num_prompts, owners_ref, terms_ref, _, out_ref):
    count = terms_ref.shape[0]
    total = out_ref.shape[1]
    rows = total // num_prompts
    row_ids = lax.broadcasted_iota(jnp.int32, (total, count), 0)
    col_ids = lax.broadcasted_iota(jnp.int32, (total, count), 1)
    hit = (owners_ref[...] == row_ids // rows) & (row_ids % rows == col_ids % rows)
    sums = nn_dot(jnp.where(hit, 1.0, 0.0).astype(BF16), terms_ref[...]).astype(BF16)
    out_ref[...] = jnp.broadcast_to(sums[None], out_ref.shape)


def add_by_prompt(owners, terms, after, num_prompts, rows, copies):
    return pl.pallas_call(
        functools.partial(add_kernel, num_prompts),
        out_shape=jax.ShapeDtypeStruct((copies, rows * num_prompts, HD), BF16),
        in_specs=[VMEM, VMEM, pl.BlockSpec(memory_space=pl.ANY)],
        out_specs=VMEM,
        compiler_params=params(4),
    )(owners, terms, after)


def place_kernel(parts_ref, key_ref, value_ref):
    prompts, own, _ = key_ref.shape
    blocks = parts_ref.shape[0] // (2 * KVH)
    rows = own // blocks
    size = prompts * own
    to = lax.broadcasted_iota(jnp.int32, (size, size), 0)
    at = lax.broadcasted_iota(jnp.int32, (size, size), 1)
    prompt, row = to // own, to % own
    hit = at == (row // rows) * (rows * prompts) + prompt * rows + row % rows
    move = jnp.where(hit, 1.0, 0.0).astype(BF16)
    for k in range(KVH):
        for side, out_ref in enumerate((key_ref, value_ref)):
            first = (k * 2 + side) * blocks
            block = parts_ref[first : first + blocks].reshape(size, HD)
            out_ref[:, :, k * HD : (k + 1) * HD] = nn_dot(move, block).reshape(
                prompts, own, HD
            )


def place(parts, shape):
    return pl.pallas_call(
        place_kernel,
        out_shape=(jax.ShapeDtypeStruct(shape, F32), jax.ShapeDtypeStruct(shape, F32)),
        in_specs=[VMEM],
        out_specs=(VMEM, VMEM),
        compiler_params=params(4),
    )(parts)


def shards(query, resp_keys, resp_values, prompt_keys, prompt_values, out_grad, group, lengths):
    places, chips = lax.axis_size("prompt"), lax.axis_size("chip")
    num_prompts, own, width = prompt_keys.shape
    wanted = pick(group, prompt_keys, prompt_values, places)
    front = lax.all_to_all(wanted, "prompt", 0, 0)
    query, grad, keys, values = query[0], out_grad[0], resp_keys[0], resp_values[0]
    stats = own_stats(lengths, query, grad, keys, values)
    front_grad, full = front_part(lengths, query, grad, front, stats)
    rows = 2 * own * width // (chips * HD)
    terms = lax.all_to_all(
        front_grad.reshape(places * chips, rows, HD), ("prompt", "chip"), 0, 0
    )
    query_grad, key_grad, value_grad = rest_part(
        lengths, query, grad, keys, values, front, full
    )
    terms = lax.all_gather(terms, "core", axis=0).reshape(-1, HD)
    owners = jnp.repeat(jnp.transpose(group.reshape(-1, CORES)).reshape(-1), rows)
    sums = add_by_prompt(owners[None], terms, key_grad, num_prompts, rows, chips)
    parts = lax.all_to_all(sums, "chip", 0, 0)
    prompt_key_grad, prompt_value_grad = place(parts, prompt_keys.shape)
    return (
        query_grad[None],
        key_grad[None],
        value_grad[None],
        prompt_key_grad,
        prompt_value_grad,
    )


def solution(mesh):
    places, resps = mesh.devices.shape
    mesh = Mesh(
        mesh.devices.reshape(places, resps // CORES, CORES), ("prompt", "chip", "core")
    )
    every = ("prompt", "chip", "core")
    row = P(every, None, None)
    front = P(None, "prompt", None)
    return jax.shard_map(
        shards,
        mesh=mesh,
        in_specs=(row, row, row, front, front, row, P(), P(every)),
        out_specs=(row, row, row, front, front),
        check_vma=False,
    )
```

```python
import functools
import math

import jax
import jax.numpy as jnp
import numpy as np
from jax import lax
from jax.experimental import pallas as pl
from jax.experimental.pallas import tpu as pltpu
from jax.sharding import Mesh
from jax.sharding import PartitionSpec as P

HD = 128
KVH = 4
GROUP = 4
CORES = 2
HALF = 128
SCALE = 1.0 / math.sqrt(HD)
LOG2E = math.log2(math.e)
PLACES = (4, 4)
CHIPS = (2, 8)
LATE_PLACE = (2, 3)
LATE_CHIP = (0, 4)
BF16 = jnp.bfloat16
F32 = jnp.float32
SMEM = pl.BlockSpec(memory_space=pltpu.SMEM)
VMEM = pl.BlockSpec(memory_space=pltpu.VMEM)


def ring(a, b, size):
    return min((a - b) % size, (b - a) % size)


def hops(a, b, sizes, steps):
    return sum(ring(i, j, n) * step for i, j, n, step in zip(a, b, sizes, steps))


def far_first(sizes, steps, root):
    members = [(i, j) for i in range(sizes[0]) for j in range(sizes[1])]
    members.sort(key=lambda m: (m != root, -hops(m, root, sizes, steps)))
    return [i * sizes[1] + j for i, j in members]


PLACE_ORDER = far_first(PLACES, (1, 2), LATE_PLACE)
CHIP_ORDER = far_first(CHIPS, (1, 1), LATE_CHIP)
NEAR_ORDER = [c ^ CHIP_ORDER[0] for c in range(len(CHIP_ORDER))]
FULL_ORDER = [p * len(CHIP_ORDER) + c for p in PLACE_ORDER for c in CHIP_ORDER]


def nt_dot(a, b):
    return lax.dot_general(a, b, (((1,), (1,)), ((), ())), preferred_element_type=F32)


def nn_dot(a, b):
    return lax.dot_general(a, b, (((1,), (0,)), ((), ())), preferred_element_type=F32)


def exp_scaled(x):
    return jnp.exp2(x * (SCALE * LOG2E))


def stack_heads(block, half, k=0):
    span = slice(half * HALF, (half + 1) * HALF)
    return jnp.concatenate(
        [block[span, h * HD : (h + 1) * HD] for h in range(k * GROUP, (k + 1) * GROUP)],
        axis=0,
    )


def live_grad(grad_ref, length, half, k=0):
    grad = stack_heads(grad_ref, half, k)
    row_ids = lax.broadcasted_iota(jnp.int32, grad.shape, 0) % HALF
    return jnp.where(row_ids + half * HALF < length, grad, jnp.zeros_like(grad))


def causal(scores):
    reach, wide = scores.shape
    key_ids = lax.broadcasted_iota(jnp.int32, (HALF, wide), 0)
    row_ids = lax.broadcasted_iota(jnp.int32, (HALF, wide), 1) % HALF
    last = jnp.where(key_ids <= row_ids, scores[reach - HALF :], -1e30)
    if reach == HALF:
        return last
    return jnp.concatenate([scores[: reach - HALF], last], axis=0)


def front_parts(front_ref, k=0):
    shards_n, both, _ = front_ref.shape
    front = front_ref[:, :, k * HD : (k + 1) * HD].astype(F32)
    keys, values = front[:, : both // 2], front[:, both // 2 :]
    return (
        keys.reshape(shards_n * both // 2, HD).astype(BF16),
        values.reshape(shards_n * both // 2, HD).astype(BF16),
    )


def pick_kernel(
    group_hbm, keys_hbm, values_hbm, out_ref, group_ref, keys_ref, values_ref, sems
):
    copies = [
        pltpu.make_async_copy(source, target, sems.at[i])
        for i, (source, target) in enumerate(
            zip((group_hbm, keys_hbm, values_hbm), (group_ref, keys_ref, values_ref))
        )
    ]
    for copy in copies:
        copy.start()
    for copy in copies:
        copy.wait()
    place_along = lax.axis_index("chip") * CORES + lax.axis_index("core")
    stride = group_ref.shape[0] // out_ref.shape[0]
    for i, place in enumerate(PLACE_ORDER):
        owner = group_ref[place * stride + place_along]
        both = jnp.concatenate(
            [keys_ref[owner].astype(F32), values_ref[owner].astype(F32)], axis=0
        )
        out_ref[i] = both.astype(BF16)


def pick(group, keys, values, count):
    _, rows, width = keys.shape
    return pl.pallas_call(
        pick_kernel,
        out_shape=jax.ShapeDtypeStruct((count, 2 * rows, width), BF16),
        in_specs=[pl.BlockSpec(memory_space=pltpu.HBM)] * 3,
        out_specs=VMEM,
        scratch_shapes=[
            pltpu.SMEM(group.shape, group.dtype),
            pltpu.VMEM(keys.shape, keys.dtype),
            pltpu.VMEM(values.shape, values.dtype),
            pltpu.SemaphoreType.DMA((3,)),
        ],
        compiler_params=params(56),
    )(group, keys, values)


def own_kernel(length_ref, query_ref, grad_ref, keys_ref, values_ref, stats_ref):
    length = length_ref[0]
    for k in range(KVH):
        features = slice(k * HD, (k + 1) * HD)
        for half in range(query_ref.shape[0] // HALF):
            reach = (half + 1) * HALF
            query = stack_heads(query_ref, half, k)
            grad = live_grad(grad_ref, length, half, k)
            scores = causal(nt_dot(keys_ref[:reach, features], query))
            top = jnp.max(scores, axis=0, keepdims=True)
            weights = exp_scaled(scores - top)
            dprob = nt_dot(values_ref[:reach, features], grad)
            total = jnp.sum(weights, axis=0, keepdims=True)
            dot = jnp.sum(weights * dprob, axis=0, keepdims=True)
            fill = jnp.zeros((5, top.shape[1]), F32)
            stats_ref[k, half] = jnp.concatenate([top, total, dot, fill], axis=0)


def front_kernel(
    length_ref, query_ref, grad_ref, front_ref, stats_ref, front_grad_ref, full_ref
):
    length = length_ref[0]
    shards_n, _, both, _ = front_grad_ref.shape
    for k in range(KVH):
        keys, values = front_parts(front_ref, k)
        key_total, value_total = 0.0, 0.0
        for half in range(query_ref.shape[0] // HALF):
            query = stack_heads(query_ref, half, k)
            grad = live_grad(grad_ref, length, half, k)
            stats = stats_ref[k, half]
            own_top, own_total, own_dot = stats[0:1], stats[1:2], stats[2:3]
            scores = nt_dot(keys, query)
            top = jnp.maximum(jnp.max(scores, axis=0, keepdims=True), own_top)
            weights = exp_scaled(scores - top)
            rescale = exp_scaled(own_top - top)
            total = jnp.sum(weights, axis=0, keepdims=True) + own_total * rescale
            inverse = 1.0 / total
            prob = weights * inverse
            prob_low = prob.astype(BF16)
            dprob = nt_dot(values, grad)
            delta = jnp.sum(prob * dprob, axis=0, keepdims=True) + own_dot * (
                rescale * inverse
            )
            dscore = (prob * (dprob - delta)).astype(BF16)
            key_total = key_total + nn_dot(dscore, query)
            value_total = value_total + nn_dot(prob_low, grad)
            fill = jnp.zeros((5, top.shape[1]), F32)
            full_ref[k, half] = jnp.concatenate([top, inverse, delta, fill], axis=0)
        front_grad_ref[:, k] = jnp.concatenate(
            [
                (key_total * SCALE).reshape(shards_n, both // 2, HD),
                value_total.reshape(shards_n, both // 2, HD),
            ],
            axis=1,
        ).astype(BF16)


def rest_kernel(
    length_ref,
    query_ref,
    grad_ref,
    keys_ref,
    values_ref,
    front_ref,
    full_ref,
    query_grad_ref,
    key_grad_ref,
    value_grad_ref,
):
    length = length_ref[0]
    front_keys, front_values = front_parts(front_ref)
    front_len = front_keys.shape[0]
    all_keys = jnp.concatenate([front_keys, keys_ref[...]], axis=0)
    all_values = jnp.concatenate([front_values, values_ref[...]], axis=0)
    keys_across = jnp.transpose(all_keys)
    key_total, value_total = None, None
    for half in range(query_ref.shape[0] // HALF):
        reach = front_len + (half + 1) * HALF
        span = slice(half * HALF, (half + 1) * HALF)
        query = stack_heads(query_ref, half)
        grad = live_grad(grad_ref, length, half)
        full = full_ref[half]
        top, inverse, delta = full[0:1], full[1:2], full[2:3]
        scores = causal(nt_dot(all_keys[:reach], query))
        prob = exp_scaled(scores - top) * inverse
        dprob = nt_dot(all_values[:reach], grad)
        dscore = (prob * (dprob - delta)).astype(BF16)
        query_term = nn_dot(keys_across[:, :reach], dscore) * SCALE
        for g in range(GROUP):
            query_grad_ref[span, g * HD : (g + 1) * HD] = jnp.transpose(
                query_term[:, g * HALF : (g + 1) * HALF]
            ).astype(BF16)
        key_term = nn_dot(dscore[front_len:], query)
        value_term = nn_dot(prob[front_len:].astype(BF16), grad)
        if key_total is None:
            key_total, value_total = key_term, value_term
        else:
            done = key_total.shape[0]
            key_total = jnp.concatenate(
                [key_total + key_term[:done], key_term[done:]], axis=0
            )
            value_total = jnp.concatenate(
                [value_total + value_term[:done], value_term[done:]], axis=0
            )
    key_grad_ref[...] = (key_total * SCALE).astype(BF16)
    value_grad_ref[...] = value_total.astype(BF16)


def attention_specs(rows, shards_n, both):
    wide = pl.BlockSpec((rows, GROUP * HD), lambda k: (0, k))
    narrow = pl.BlockSpec((rows, HD), lambda k: (0, k))
    front = pl.BlockSpec((shards_n, both, HD), lambda k: (0, 0, k))
    stats = pl.BlockSpec(
        (None, rows // HALF, 8, GROUP * HALF), lambda k: (k, 0, 0, 0)
    )
    return wide, narrow, front, stats


def params(mib):
    return pltpu.CompilerParams(vmem_limit_bytes=mib * 1024 * 1024)


def cost(matmuls, keys):
    flops = 2 * KVH * GROUP * 256 * keys * HD * matmuls
    return pl.CostEstimate(
        flops=flops, bytes_accessed=3 << 20, transcendentals=KVH * GROUP * 256 * keys
    )


def own_stats(length, query, grad, keys, values):
    rows = query.shape[0]
    return pl.pallas_call(
        own_kernel,
        out_shape=jax.ShapeDtypeStruct((KVH, rows // HALF, 8, GROUP * HALF), F32),
        in_specs=[SMEM, VMEM, VMEM, VMEM, VMEM],
        out_specs=VMEM,
        compiler_params=params(16),
        cost_estimate=cost(2, 256),
    )(length, query, grad, keys, values)


def front_part(length, query, grad, front, own):
    shards_n, both, _ = front.shape
    return pl.pallas_call(
        front_kernel,
        out_shape=(
            jax.ShapeDtypeStruct((shards_n, KVH, both, HD), BF16),
            jax.ShapeDtypeStruct(own.shape, F32),
        ),
        in_specs=[SMEM, VMEM, VMEM, VMEM, VMEM],
        out_specs=(VMEM, VMEM),
        compiler_params=params(16),
        cost_estimate=cost(4, 128),
    )(length, query, grad, front, own)


def rest_part(length, query, grad, keys, values, front, full):
    shards_n, both, _ = front.shape
    wide, narrow, front_spec, stats = attention_specs(query.shape[0], shards_n, both)
    return pl.pallas_call(
        rest_kernel,
        grid=(KVH,),
        out_shape=(
            jax.ShapeDtypeStruct(query.shape, BF16),
            jax.ShapeDtypeStruct(keys.shape, BF16),
            jax.ShapeDtypeStruct(values.shape, BF16),
        ),
        in_specs=[SMEM, wide, wide, narrow, narrow, front_spec, stats],
        out_specs=(wide, narrow, narrow),
        compiler_params=params(24),
        cost_estimate=cost(5, 384),
    )(length, query, grad, keys, values, front, full)


def owners_kernel(rows, group_ref, slots_ref, out_ref):
    count, size = group_ref.shape[1], slots_ref.shape[1]
    hit = lax.broadcasted_iota(jnp.int32, (count, size), 0) == slots_ref[...]
    group = jnp.broadcast_to(group_ref[...].astype(F32).astype(BF16), (8, count))
    out = nn_dot(group, jnp.where(hit, 1.0, 0.0).astype(BF16))
    out_ref[...] = out[:1].astype(jnp.int32)


def owners_of(group, rows):
    slots = [m * CORES + core for core in range(CORES) for m in FULL_ORDER]
    slots = np.repeat(np.array(slots, np.int32), rows)[None]
    return pl.pallas_call(
        functools.partial(owners_kernel, rows),
        out_shape=jax.ShapeDtypeStruct(slots.shape, jnp.int32),
        in_specs=[VMEM, VMEM],
        out_specs=VMEM,
        compiler_params=params(8),
    )(group[None], slots)


def add_kernel(num_prompts, owners_ref, terms_ref, _, out_ref):
    count = terms_ref.shape[0]
    total = out_ref.shape[1]
    rows = total // num_prompts
    row_ids = lax.broadcasted_iota(jnp.int32, (total, count), 0)
    col_ids = lax.broadcasted_iota(jnp.int32, (total, count), 1)
    hit = (owners_ref[...] == row_ids // rows) & (row_ids % rows == col_ids % rows)
    sums = nn_dot(jnp.where(hit, 1.0, 0.0).astype(BF16), terms_ref[...]).astype(BF16)
    out_ref[...] = jnp.broadcast_to(sums[None], out_ref.shape)


def add_by_prompt(owners, terms, after, num_prompts, rows, copies):
    return pl.pallas_call(
        functools.partial(add_kernel, num_prompts),
        out_shape=jax.ShapeDtypeStruct((copies, rows * num_prompts, HD), BF16),
        in_specs=[VMEM, VMEM, pl.BlockSpec(memory_space=pl.ANY)],
        out_specs=VMEM,
        compiler_params=params(4),
    )(owners, terms, after)


def place_kernel(parts_ref, key_ref, value_ref):
    came = [NEAR_ORDER.index(chip) for chip in CHIP_ORDER]
    prompts, own, _ = key_ref.shape
    blocks = parts_ref.shape[0] // (2 * KVH)
    rows = own // blocks
    size = prompts * own
    to = lax.broadcasted_iota(jnp.int32, (size, size), 0)
    at = lax.broadcasted_iota(jnp.int32, (size, size), 1)
    prompt, row = to // own, to % own
    hit = at == (row // rows) * (rows * prompts) + prompt * rows + row % rows
    move = jnp.where(hit, 1.0, 0.0).astype(BF16)
    for k in range(KVH):
        for side, out_ref in enumerate((key_ref, value_ref)):
            first = (k * 2 + side) * blocks
            block = jnp.concatenate(
                [parts_ref[came[first + w]] for w in range(blocks)], axis=0
            )
            out_ref[:, :, k * HD : (k + 1) * HD] = nn_dot(move, block).reshape(
                prompts, own, HD
            )


def place(parts, shape):
    return pl.pallas_call(
        place_kernel,
        out_shape=(jax.ShapeDtypeStruct(shape, F32), jax.ShapeDtypeStruct(shape, F32)),
        in_specs=[VMEM],
        out_specs=(VMEM, VMEM),
        compiler_params=params(4),
    )(parts)


def exchange(blocks, axes, order):
    return lax.all_to_all(blocks, axes, 0, 0, axis_index_groups=[order])


def shards(query, resp_keys, resp_values, prompt_keys, prompt_values, out_grad, group, lengths):
    places, chips = lax.axis_size("prompt"), lax.axis_size("chip")
    num_prompts, own, width = prompt_keys.shape
    wanted = pick(group, prompt_keys, prompt_values, places)
    front = exchange(wanted, "prompt", PLACE_ORDER)
    query, grad, keys, values = query[0], out_grad[0], resp_keys[0], resp_values[0]
    stats = own_stats(lengths, query, grad, keys, values)
    front_grad, full = front_part(lengths, query, grad, front, stats)
    rows = 2 * own * width // (chips * HD)
    terms = exchange(
        front_grad.reshape(places * chips, rows, HD), ("prompt", "chip"), FULL_ORDER
    )
    query_grad, key_grad, value_grad = rest_part(
        lengths, query, grad, keys, values, front, full
    )
    terms = lax.all_gather(terms, "core", axis=0).reshape(-1, HD)
    owners = owners_of(group, rows)
    sums = add_by_prompt(owners, terms, key_grad, num_prompts, rows, chips)
    parts = exchange(sums, "chip", NEAR_ORDER)
    prompt_key_grad, prompt_value_grad = place(parts, prompt_keys.shape)
    return (
        query_grad[None],
        key_grad[None],
        value_grad[None],
        prompt_key_grad,
        prompt_value_grad,
    )


def solution(mesh):
    places, resps = mesh.devices.shape
    mesh = Mesh(
        mesh.devices.reshape(places, resps // CORES, CORES), ("prompt", "chip", "core")
    )
    every = ("prompt", "chip", "core")
    row = P(every, None, None)
    front = P(None, "prompt", None)
    return jax.shard_map(
        shards,
        mesh=mesh,
        in_specs=(row, row, row, front, front, row, P(), P(every)),
        out_specs=(row, row, row, front, front),
        check_vma=False,
    )
```

```python
import functools
import math

import jax
import jax.numpy as jnp
import numpy as np
from jax import lax
from jax.experimental import pallas as pl
from jax.experimental.pallas import tpu as pltpu
from jax.sharding import Mesh
from jax.sharding import PartitionSpec as P

HD = 128
KVH = 4
GROUP = 4
CORES = 2
HALF = 128
SCALE = 1.0 / math.sqrt(HD)
LOG2E = math.log2(math.e)
PLACES = (4, 4)
CHIPS = (2, 8)
LATE_PLACE = (2, 2)
LATE_CHIP = (0, 4)
BF16 = jnp.bfloat16
F32 = jnp.float32
SMEM = pl.BlockSpec(memory_space=pltpu.SMEM)
VMEM = pl.BlockSpec(memory_space=pltpu.VMEM)
HBM = pl.BlockSpec(memory_space=pltpu.HBM)


def ring(a, b, size):
    return min((a - b) % size, (b - a) % size)


def hops(a, b, sizes, steps):
    return sum(ring(i, j, n) * step for i, j, n, step in zip(a, b, sizes, steps))


def far_first(sizes, steps, root):
    members = [(i, j) for i in range(sizes[0]) for j in range(sizes[1])]
    members.sort(key=lambda m: (m != root, -hops(m, root, sizes, steps)))
    return [i * sizes[1] + j for i, j in members]


PLACE_ORDER = far_first(PLACES, (1, 2), LATE_PLACE)
CHIP_ORDER = far_first(CHIPS, (1, 1), LATE_CHIP)
NEAR_ORDER = [c ^ CHIP_ORDER[0] for c in range(len(CHIP_ORDER))]
FULL_ORDER = [p * len(CHIP_ORDER) + c for p in PLACE_ORDER for c in CHIP_ORDER]


def nt_dot(a, b):
    return lax.dot_general(a, b, (((1,), (1,)), ((), ())), preferred_element_type=F32)


def nn_dot(a, b):
    return lax.dot_general(a, b, (((1,), (0,)), ((), ())), preferred_element_type=F32)


def exp_scaled(x):
    return jnp.exp2(x * (SCALE * LOG2E))


def stack_heads(block, half, k=0):
    span = slice(half * HALF, (half + 1) * HALF)
    return jnp.concatenate(
        [block[span, h * HD : (h + 1) * HD] for h in range(k * GROUP, (k + 1) * GROUP)],
        axis=0,
    )


def live_grad(grad_ref, length, half, k=0):
    grad = stack_heads(grad_ref, half, k)
    row_ids = lax.broadcasted_iota(jnp.int32, grad.shape, 0) % HALF
    return jnp.where(row_ids + half * HALF < length, grad, jnp.zeros_like(grad))


def causal(scores):
    reach, wide = scores.shape
    key_ids = lax.broadcasted_iota(jnp.int32, (HALF, wide), 0)
    row_ids = lax.broadcasted_iota(jnp.int32, (HALF, wide), 1) % HALF
    last = jnp.where(key_ids <= row_ids, scores[reach - HALF :], -1e30)
    if reach == HALF:
        return last
    return jnp.concatenate([scores[: reach - HALF], last], axis=0)


def front_parts(front_ref, k=0):
    shards_n, both, _ = front_ref.shape
    front = front_ref[:, :, k * HD : (k + 1) * HD].astype(F32)
    keys, values = front[:, : both // 2], front[:, both // 2 :]
    return (
        keys.reshape(shards_n * both // 2, HD).astype(BF16),
        values.reshape(shards_n * both // 2, HD).astype(BF16),
    )


def peer_chip(side, row, place):
    bent = place % PLACES[1] >= PLACES[1] // 2
    return (1 - side if bent else side) * CHIPS[1] + row


def front_groups():
    return [
        [place * len(CHIP_ORDER) + peer_chip(side, row, place) for place in PLACE_ORDER]
        for side in range(CHIPS[0])
        for row in range(CHIPS[1])
    ]


def pick_kernel(
    group_hbm, keys_hbm, values_hbm, out_ref, group_ref, keys_ref, values_ref, sems
):
    copies = [
        pltpu.make_async_copy(source, target, sems.at[i])
        for i, (source, target) in enumerate(
            zip((group_hbm, keys_hbm, values_hbm), (group_ref, keys_ref, values_ref))
        )
    ]
    for copy in copies:
        copy.start()
    chip, core = lax.axis_index("chip"), lax.axis_index("core")
    row = chip % CHIPS[1]
    bent = lax.axis_index("prompt") % PLACES[1] >= PLACES[1] // 2
    side = jnp.where(bent, 1 - chip // CHIPS[1], chip // CHIPS[1])
    for copy in copies:
        copy.wait()
    for i, place in enumerate(PLACE_ORDER):
        peer = place * len(CHIP_ORDER) + peer_chip(side, row, place)
        owner = group_ref[peer * CORES + core]
        both = jnp.concatenate(
            [keys_ref[owner].astype(F32), values_ref[owner].astype(F32)], axis=0
        )
        out_ref[i] = both.astype(BF16)


def pick(group, keys, values, count):
    _, rows, width = keys.shape
    return pl.pallas_call(
        pick_kernel,
        out_shape=jax.ShapeDtypeStruct((count, 2 * rows, width), BF16),
        in_specs=[HBM] * 3,
        out_specs=VMEM,
        scratch_shapes=[
            pltpu.SMEM(group.shape, group.dtype),
            pltpu.VMEM(keys.shape, keys.dtype),
            pltpu.VMEM(values.shape, values.dtype),
            pltpu.SemaphoreType.DMA((3,)),
        ],
        compiler_params=params(56),
    )(group, keys, values)


def own_kernel(
    length_ref,
    query_ref,
    grad_ref,
    keys_ref,
    values_ref,
    group_ref,
    slots_ref,
    stats_ref,
    owners_ref,
):
    length = length_ref[0]
    for k in range(KVH):
        features = slice(k * HD, (k + 1) * HD)
        for half in range(query_ref.shape[0] // HALF):
            reach = (half + 1) * HALF
            query = stack_heads(query_ref, half, k)
            grad = live_grad(grad_ref, length, half, k)
            scores = causal(nt_dot(keys_ref[:reach, features], query))
            top = jnp.max(scores, axis=0, keepdims=True)
            weights = exp_scaled(scores - top)
            dprob = nt_dot(values_ref[:reach, features], grad)
            total = jnp.sum(weights, axis=0, keepdims=True)
            dot = jnp.sum(weights * dprob, axis=0, keepdims=True)
            fill = jnp.zeros((5, top.shape[1]), F32)
            stats_ref[k, half] = jnp.concatenate([top, total, dot, fill], axis=0)
    count, size = group_ref.shape[1], slots_ref.shape[1]
    hit = lax.broadcasted_iota(jnp.int32, (count, size), 0) == slots_ref[...]
    group = jnp.broadcast_to(group_ref[...].astype(F32).astype(BF16), (8, count))
    owners = nn_dot(group, jnp.where(hit, 1.0, 0.0).astype(BF16))
    owners_ref[...] = owners[:1].astype(jnp.int32)


def front_kernel(
    length_ref,
    query_ref,
    grad_ref,
    front_ref,
    stats_ref,
    front_grad_hbm,
    full_ref,
    front_grad_ref,
    sems,
):
    length = length_ref[0]
    _, shards_n, both, _ = front_grad_ref.shape
    copies = [
        pltpu.make_async_copy(front_grad_ref.at[k], front_grad_hbm.at[:, k], sems.at[k])
        for k in range(KVH)
    ]
    front_len = shards_n * (both // 2)
    halves = range(query_ref.shape[0] // HALF)

    def begin(k):
        keys, values = front_parts(front_ref, k)
        query = jnp.concatenate([stack_heads(query_ref, half, k) for half in halves])
        grad = jnp.concatenate(
            [live_grad(grad_ref, length, half, k) for half in halves]
        )
        both = jnp.concatenate([query, grad], axis=1)
        none = jnp.zeros_like(keys)
        front = jnp.concatenate(
            [
                jnp.concatenate([keys, none], axis=1),
                jnp.concatenate([none, values], axis=1),
            ]
        )
        return both, nt_dot(front, both)

    ahead = begin(0)
    for k in range(KVH):
        rows, dots = ahead
        if k + 1 < KVH:
            ahead = begin(k + 1)
        scores, dprob = dots[:front_len], dots[front_len:]
        stats = jnp.concatenate([stats_ref[k, half] for half in halves], axis=1)
        own_top, own_total, own_dot = stats[0:1], stats[1:2], stats[2:3]
        top = jnp.maximum(jnp.max(scores, axis=0, keepdims=True), own_top)
        weights = exp_scaled(scores - top)
        rescale = exp_scaled(own_top - top)
        total = jnp.sum(weights, axis=0, keepdims=True) + own_total * rescale
        inverse = 1.0 / total
        prob = weights * inverse
        dots = jnp.sum(weights * dprob, axis=0, keepdims=True) + own_dot * rescale
        delta = dots * inverse
        dscore = (prob * (dprob - delta)).astype(BF16)
        sums = nn_dot(jnp.concatenate([dscore, prob.astype(BF16)]), rows)
        key_total = sums[:front_len, :HD] * SCALE
        value_total = sums[front_len:, HD:]
        fill = jnp.zeros((5, top.shape[1]), F32)
        full = jnp.concatenate([top, inverse, delta, fill], axis=0)
        for half in halves:
            full_ref[k, half] = full[:, half * GROUP * HALF : (half + 1) * GROUP * HALF]
        front_grad_ref[k] = jnp.concatenate(
            [
                key_total.reshape(shards_n, both // 2, HD),
                value_total.reshape(shards_n, both // 2, HD),
            ],
            axis=1,
        ).astype(BF16)
        copies[k].start()
    for copy in copies:
        copy.wait()


def rest_kernel(
    length_ref,
    query_ref,
    grad_ref,
    keys_ref,
    values_ref,
    front_ref,
    full_ref,
    query_grad_ref,
    key_grad_ref,
    value_grad_ref,
):
    length = length_ref[0]
    front_keys, front_values = front_parts(front_ref)
    front_len = front_keys.shape[0]
    all_keys = jnp.concatenate([front_keys, keys_ref[...]], axis=0)
    all_values = jnp.concatenate([front_values, values_ref[...]], axis=0)
    keys_across = jnp.transpose(all_keys)
    key_total, value_total = None, None
    for half in range(query_ref.shape[0] // HALF):
        reach = front_len + (half + 1) * HALF
        span = slice(half * HALF, (half + 1) * HALF)
        query = stack_heads(query_ref, half)
        grad = live_grad(grad_ref, length, half)
        full = full_ref[half]
        top, inverse, delta = full[0:1], full[1:2], full[2:3]
        scores = causal(nt_dot(all_keys[:reach], query))
        prob = exp_scaled(scores - top) * inverse
        dprob = nt_dot(all_values[:reach], grad)
        dscore = (prob * (dprob - delta)).astype(BF16)
        query_term = nn_dot(keys_across[:, :reach], dscore) * SCALE
        for g in range(GROUP):
            query_grad_ref[span, g * HD : (g + 1) * HD] = jnp.transpose(
                query_term[:, g * HALF : (g + 1) * HALF]
            ).astype(BF16)
        key_term = nn_dot(dscore[front_len:], query)
        value_term = nn_dot(prob[front_len:].astype(BF16), grad)
        if key_total is None:
            key_total, value_total = key_term, value_term
        else:
            done = key_total.shape[0]
            key_total = jnp.concatenate(
                [key_total + key_term[:done], key_term[done:]], axis=0
            )
            value_total = jnp.concatenate(
                [value_total + value_term[:done], value_term[done:]], axis=0
            )
    key_grad_ref[...] = (key_total * SCALE).astype(BF16)
    value_grad_ref[...] = value_total.astype(BF16)


def attention_specs(rows, shards_n, both):
    wide = pl.BlockSpec((rows, GROUP * HD), lambda k: (0, k))
    narrow = pl.BlockSpec((rows, HD), lambda k: (0, k))
    front = pl.BlockSpec((shards_n, both, HD), lambda k: (0, 0, k))
    stats = pl.BlockSpec(
        (None, rows // HALF, 8, GROUP * HALF), lambda k: (k, 0, 0, 0)
    )
    return wide, narrow, front, stats


def params(mib):
    return pltpu.CompilerParams(vmem_limit_bytes=mib * 1024 * 1024)


def cost(matmuls, keys):
    flops = 2 * KVH * GROUP * 256 * keys * HD * matmuls
    return pl.CostEstimate(
        flops=flops, bytes_accessed=3 << 20, transcendentals=KVH * GROUP * 256 * keys
    )


def own_stats(length, query, grad, keys, values, group, copies):
    rows = query.shape[0]
    slots = [m * CORES + core for core in range(CORES) for m in FULL_ORDER]
    slots = np.repeat(np.array(slots, np.int32), copies)[None]
    return pl.pallas_call(
        own_kernel,
        out_shape=(
            jax.ShapeDtypeStruct((KVH, rows // HALF, 8, GROUP * HALF), F32),
            jax.ShapeDtypeStruct(slots.shape, jnp.int32),
        ),
        in_specs=[SMEM] + [VMEM] * 6,
        out_specs=(VMEM, VMEM),
        compiler_params=params(16),
        cost_estimate=cost(2, 256),
    )(length, query, grad, keys, values, group[None], slots)


def front_part(length, query, grad, front, own):
    shards_n, both, _ = front.shape
    return pl.pallas_call(
        front_kernel,
        out_shape=(
            jax.ShapeDtypeStruct((shards_n, KVH, both, HD), BF16),
            jax.ShapeDtypeStruct(own.shape, F32),
        ),
        in_specs=[SMEM, VMEM, VMEM, VMEM, VMEM],
        out_specs=(HBM, VMEM),
        scratch_shapes=[
            pltpu.VMEM((KVH, shards_n, both, HD), BF16),
            pltpu.SemaphoreType.DMA((KVH,)),
        ],
        compiler_params=params(16),
        cost_estimate=cost(4, 128),
    )(length, query, grad, front, own)


def rest_part(length, query, grad, keys, values, front, full):
    shards_n, both, _ = front.shape
    wide, narrow, front_spec, stats = attention_specs(query.shape[0], shards_n, both)
    return pl.pallas_call(
        rest_kernel,
        grid=(KVH,),
        out_shape=(
            jax.ShapeDtypeStruct(query.shape, BF16),
            jax.ShapeDtypeStruct(keys.shape, BF16),
            jax.ShapeDtypeStruct(values.shape, BF16),
        ),
        in_specs=[SMEM, wide, wide, narrow, narrow, front_spec, stats],
        out_specs=(wide, narrow, narrow),
        compiler_params=params(24),
        cost_estimate=cost(5, 384),
    )(length, query, grad, keys, values, front, full)


def add_kernel(num_prompts, owners_ref, terms_ref, _, out_ref):
    count = terms_ref.shape[0]
    total = out_ref.shape[1]
    rows = total // num_prompts
    row_ids = lax.broadcasted_iota(jnp.int32, (total, count), 0)
    col_ids = lax.broadcasted_iota(jnp.int32, (total, count), 1)
    hit = (owners_ref[...] == row_ids // rows) & (row_ids % rows == col_ids % rows)
    sums = nn_dot(jnp.where(hit, 1.0, 0.0).astype(BF16), terms_ref[...]).astype(BF16)
    out_ref[...] = jnp.broadcast_to(sums[None], out_ref.shape)


def add_by_prompt(owners, terms, after, num_prompts, rows, copies):
    return pl.pallas_call(
        functools.partial(add_kernel, num_prompts),
        out_shape=jax.ShapeDtypeStruct((copies, rows * num_prompts, HD), BF16),
        in_specs=[VMEM, VMEM, pl.BlockSpec(memory_space=pl.ANY)],
        out_specs=VMEM,
        compiler_params=params(4),
    )(owners, terms, after)


def place_kernel(parts_ref, key_hbm, value_hbm, out_ref, sems):
    came = [NEAR_ORDER.index(chip) for chip in CHIP_ORDER]
    _, prompts, own, _ = out_ref.shape
    blocks = parts_ref.shape[0] // (2 * KVH)
    rows = own // blocks
    size = prompts * own
    to = lax.broadcasted_iota(jnp.int32, (size, size), 0)
    at = lax.broadcasted_iota(jnp.int32, (size, size), 1)
    prompt, row = to // own, to % own
    hit = at == (row // rows) * (rows * prompts) + prompt * rows + row % rows
    move = jnp.where(hit, 1.0, 0.0).astype(BF16)
    copies = []
    for side, out_hbm in enumerate((key_hbm, value_hbm)):
        for k in range(KVH):
            first = (k * 2 + side) * blocks
            block = jnp.concatenate(
                [parts_ref[came[first + w]] for w in range(blocks)], axis=0
            )
            out_ref[side, :, :, k * HD : (k + 1) * HD] = nn_dot(move, block).reshape(
                prompts, own, HD
            )
        copies.append(pltpu.make_async_copy(out_ref.at[side], out_hbm, sems.at[side]))
        copies[-1].start()
    for copy in copies:
        copy.wait()


def place(parts, shape):
    return pl.pallas_call(
        place_kernel,
        out_shape=(jax.ShapeDtypeStruct(shape, F32), jax.ShapeDtypeStruct(shape, F32)),
        in_specs=[VMEM],
        out_specs=(HBM, HBM),
        scratch_shapes=[
            pltpu.VMEM((2,) + shape, F32),
            pltpu.SemaphoreType.DMA((2,)),
        ],
        compiler_params=params(4),
    )(parts)


def exchange(blocks, axes, groups):
    return lax.all_to_all(blocks, axes, 0, 0, axis_index_groups=groups)


def shards(query, resp_keys, resp_values, prompt_keys, prompt_values, out_grad, group, lengths):
    places, chips = lax.axis_size("prompt"), lax.axis_size("chip")
    num_prompts, own, width = prompt_keys.shape
    wanted = pick(group, prompt_keys, prompt_values, places)
    front = exchange(wanted, ("prompt", "chip"), front_groups())
    query, grad, keys, values = query[0], out_grad[0], resp_keys[0], resp_values[0]
    rows = 2 * own * width // (chips * HD)
    stats, owners = own_stats(lengths, query, grad, keys, values, group, rows)
    front_grad, full = front_part(lengths, query, grad, front, stats)
    terms = exchange(
        front_grad.reshape(places * chips, rows, HD), ("prompt", "chip"), [FULL_ORDER]
    )
    query_grad, key_grad, value_grad = rest_part(
        lengths, query, grad, keys, values, front, full
    )
    terms = lax.all_gather(terms, "core", axis=0).reshape(-1, HD)
    sums = add_by_prompt(owners, terms, key_grad, num_prompts, rows, chips)
    parts = exchange(sums, "chip", [NEAR_ORDER])
    prompt_key_grad, prompt_value_grad = place(parts, prompt_keys.shape)
    return (
        query_grad[None],
        key_grad[None],
        value_grad[None],
        prompt_key_grad,
        prompt_value_grad,
    )


def solution(mesh):
    places, resps = mesh.devices.shape
    mesh = Mesh(
        mesh.devices.reshape(places, resps // CORES, CORES), ("prompt", "chip", "core")
    )
    every = ("prompt", "chip", "core")
    row = P(every, None, None)
    front = P(None, "prompt", None)
    return jax.shard_map(
        shards,
        mesh=mesh,
        in_specs=(row, row, row, front, front, row, P(), P(every)),
        out_specs=(row, row, row, front, front),
        check_vma=False,
    )
```

```python
import functools
import math

import jax
import jax.numpy as jnp
import numpy as np
from jax import lax
from jax.experimental import pallas as pl
from jax.experimental.pallas import tpu as pltpu
from jax.sharding import Mesh
from jax.sharding import PartitionSpec as P

HD = 128
KVH = 4
GROUP = 4
CORES = 2
HALF = 128
SCALE = 1.0 / math.sqrt(HD)
LOG2E = math.log2(math.e)
PLACES = (4, 4)
CHIPS = (2, 8)
LATE_PLACE = (2, 2)
LATE_CHIP = (0, 4)
BF16 = jnp.bfloat16
F32 = jnp.float32
SMEM = pl.BlockSpec(memory_space=pltpu.SMEM)
VMEM = pl.BlockSpec(memory_space=pltpu.VMEM)
HBM = pl.BlockSpec(memory_space=pltpu.HBM)


def ring(a, b, size):
    return min((a - b) % size, (b - a) % size)


def hops(a, b, sizes, steps):
    return sum(ring(i, j, n) * step for i, j, n, step in zip(a, b, sizes, steps))


def far_first(sizes, steps, root):
    members = [(i, j) for i in range(sizes[0]) for j in range(sizes[1])]
    members.sort(key=lambda m: (m != root, -hops(m, root, sizes, steps)))
    return [i * sizes[1] + j for i, j in members]


PLACE_ORDER = far_first(PLACES, (1, 2), LATE_PLACE)
CHIP_ORDER = far_first(CHIPS, (1, 1), LATE_CHIP)
NEAR_ORDER = [c ^ CHIP_ORDER[0] for c in range(len(CHIP_ORDER))]
FULL_ORDER = [p * len(CHIP_ORDER) + c for p in PLACE_ORDER for c in CHIP_ORDER]


def nt_dot(a, b):
    return lax.dot_general(a, b, (((1,), (1,)), ((), ())), preferred_element_type=F32)


def nn_dot(a, b):
    return lax.dot_general(a, b, (((1,), (0,)), ((), ())), preferred_element_type=F32)


def exp_scaled(x):
    return jnp.exp2(x * (SCALE * LOG2E))


def stack_heads(block, half, k=0):
    span = slice(half * HALF, (half + 1) * HALF)
    return jnp.concatenate(
        [block[span, h * HD : (h + 1) * HD] for h in range(k * GROUP, (k + 1) * GROUP)],
        axis=0,
    )


def live_grad(grad_ref, length, half, k=0):
    grad = stack_heads(grad_ref, half, k)
    row_ids = lax.broadcasted_iota(jnp.int32, grad.shape, 0) % HALF
    return jnp.where(row_ids + half * HALF < length, grad, jnp.zeros_like(grad))


def causal(scores):
    reach, wide = scores.shape
    key_ids = lax.broadcasted_iota(jnp.int32, (HALF, wide), 0)
    row_ids = lax.broadcasted_iota(jnp.int32, (HALF, wide), 1) % HALF
    last = jnp.where(key_ids <= row_ids, scores[reach - HALF :], -1e30)
    if reach == HALF:
        return last
    return jnp.concatenate([scores[: reach - HALF], last], axis=0)


def front_parts(front_ref, k=0):
    shards_n, both, _ = front_ref.shape
    front = front_ref[:, :, k * HD : (k + 1) * HD].astype(F32)
    keys, values = front[:, : both // 2], front[:, both // 2 :]
    return (
        keys.reshape(shards_n * both // 2, HD).astype(BF16),
        values.reshape(shards_n * both // 2, HD).astype(BF16),
    )


def peer_chip(side, row, place):
    bent = place % PLACES[1] >= PLACES[1] // 2
    return (1 - side if bent else side) * CHIPS[1] + row


def front_groups():
    return [
        [place * len(CHIP_ORDER) + peer_chip(side, row, place) for place in PLACE_ORDER]
        for side in range(CHIPS[0])
        for row in range(CHIPS[1])
    ]


def pick_kernel(
    group_hbm, keys_hbm, values_hbm, out_ref, group_ref, keys_ref, values_ref, sems
):
    copies = [
        pltpu.make_async_copy(source, target, sems.at[i])
        for i, (source, target) in enumerate(
            zip((group_hbm, keys_hbm, values_hbm), (group_ref, keys_ref, values_ref))
        )
    ]
    for copy in copies:
        copy.start()
    chip, core = lax.axis_index("chip"), lax.axis_index("core")
    row = chip % CHIPS[1]
    bent = lax.axis_index("prompt") % PLACES[1] >= PLACES[1] // 2
    side = jnp.where(bent, 1 - chip // CHIPS[1], chip // CHIPS[1])
    for copy in copies:
        copy.wait()
    for i, place in enumerate(PLACE_ORDER):
        peer = place * len(CHIP_ORDER) + peer_chip(side, row, place)
        owner = group_ref[peer * CORES + core]
        both = jnp.concatenate(
            [keys_ref[owner].astype(F32), values_ref[owner].astype(F32)], axis=0
        )
        out_ref[i] = both.astype(BF16)


def pick(group, keys, values, count):
    _, rows, width = keys.shape
    return pl.pallas_call(
        pick_kernel,
        out_shape=jax.ShapeDtypeStruct((count, 2 * rows, width), BF16),
        in_specs=[HBM] * 3,
        out_specs=VMEM,
        scratch_shapes=[
            pltpu.SMEM(group.shape, group.dtype),
            pltpu.VMEM(keys.shape, keys.dtype),
            pltpu.VMEM(values.shape, values.dtype),
            pltpu.SemaphoreType.DMA((3,)),
        ],
        compiler_params=params(56),
    )(group, keys, values)


def own_kernel(
    length_ref,
    query_ref,
    grad_ref,
    keys_ref,
    values_ref,
    group_ref,
    slots_ref,
    stats_ref,
    owners_ref,
):
    length = length_ref[0]
    for k in range(KVH):
        features = slice(k * HD, (k + 1) * HD)
        for half in range(query_ref.shape[0] // HALF):
            reach = (half + 1) * HALF
            query = stack_heads(query_ref, half, k)
            grad = live_grad(grad_ref, length, half, k)
            scores = causal(nt_dot(keys_ref[:reach, features], query))
            top = jnp.max(scores, axis=0, keepdims=True)
            weights = exp_scaled(scores - top)
            dprob = nt_dot(values_ref[:reach, features], grad)
            total = jnp.sum(weights, axis=0, keepdims=True)
            dot = jnp.sum(weights * dprob, axis=0, keepdims=True)
            fill = jnp.zeros((5, top.shape[1]), F32)
            stats_ref[k, half] = jnp.concatenate([top, total, dot, fill], axis=0)
    count, size = group_ref.shape[1], slots_ref.shape[1]
    hit = lax.broadcasted_iota(jnp.int32, (count, size), 0) == slots_ref[...]
    group = jnp.broadcast_to(group_ref[...].astype(F32).astype(BF16), (8, count))
    owners = nn_dot(group, jnp.where(hit, 1.0, 0.0).astype(BF16))
    owners_ref[...] = owners[:1].astype(jnp.int32)


def front_kernel(
    length_ref,
    query_ref,
    grad_ref,
    front_ref,
    stats_ref,
    front_grad_hbm,
    full_ref,
    front_grad_ref,
    sems,
):
    length = length_ref[0]
    _, shards_n, both, _ = front_grad_ref.shape
    copies = [
        pltpu.make_async_copy(front_grad_ref.at[k], front_grad_hbm.at[:, k], sems.at[k])
        for k in range(KVH)
    ]
    front_len = shards_n * (both // 2)
    halves = range(query_ref.shape[0] // HALF)

    def begin(k):
        keys, values = front_parts(front_ref, k)
        query = jnp.concatenate([stack_heads(query_ref, half, k) for half in halves])
        grad = jnp.concatenate(
            [live_grad(grad_ref, length, half, k) for half in halves]
        )
        both = jnp.concatenate([query, grad], axis=1)
        none = jnp.zeros_like(keys)
        front = jnp.concatenate(
            [
                jnp.concatenate([keys, none], axis=1),
                jnp.concatenate([none, values], axis=1),
            ]
        )
        return both, nt_dot(front, both)

    ahead = begin(0)
    for k in range(KVH):
        rows, dots = ahead
        if k + 1 < KVH:
            ahead = begin(k + 1)
        scores, dprob = dots[:front_len], dots[front_len:]
        stats = jnp.concatenate([stats_ref[k, half] for half in halves], axis=1)
        own_top, own_total, own_dot = stats[0:1], stats[1:2], stats[2:3]
        top = jnp.maximum(jnp.max(scores, axis=0, keepdims=True), own_top)
        weights = exp_scaled(scores - top)
        rescale = exp_scaled(own_top - top)
        total = jnp.sum(weights, axis=0, keepdims=True) + own_total * rescale
        inverse = 1.0 / total
        prob = weights * inverse
        dots = jnp.sum(weights * dprob, axis=0, keepdims=True) + own_dot * rescale
        delta = dots * inverse
        dscore = (prob * (dprob - delta)).astype(BF16)
        sums = nn_dot(jnp.concatenate([dscore, prob.astype(BF16)]), rows)
        key_total = sums[:front_len, :HD] * SCALE
        value_total = sums[front_len:, HD:]
        fill = jnp.zeros((5, top.shape[1]), F32)
        full = jnp.concatenate([top, inverse, delta, fill], axis=0)
        for half in halves:
            full_ref[k, half] = full[:, half * GROUP * HALF : (half + 1) * GROUP * HALF]
        front_grad_ref[k] = jnp.concatenate(
            [
                key_total.reshape(shards_n, both // 2, HD),
                value_total.reshape(shards_n, both // 2, HD),
            ],
            axis=1,
        ).astype(BF16)
        copies[k].start()
    for copy in copies:
        copy.wait()


def rest_kernel(
    length_ref,
    query_ref,
    grad_ref,
    keys_ref,
    values_ref,
    front_ref,
    full_ref,
    query_grad_ref,
    key_grad_ref,
    value_grad_ref,
    done_ref,
):
    done_ref[...] = jnp.zeros_like(done_ref)
    length = length_ref[0]
    front_keys, front_values = front_parts(front_ref)
    front_len = front_keys.shape[0]
    all_keys = jnp.concatenate([front_keys, keys_ref[...]], axis=0)
    all_values = jnp.concatenate([front_values, values_ref[...]], axis=0)
    keys_across = jnp.transpose(all_keys)
    key_total, value_total = None, None
    for half in range(query_ref.shape[0] // HALF):
        reach = front_len + (half + 1) * HALF
        span = slice(half * HALF, (half + 1) * HALF)
        query = stack_heads(query_ref, half)
        grad = live_grad(grad_ref, length, half)
        full = full_ref[half]
        top, inverse, delta = full[0:1], full[1:2], full[2:3]
        scores = causal(nt_dot(all_keys[:reach], query))
        prob = exp_scaled(scores - top) * inverse
        dprob = nt_dot(all_values[:reach], grad)
        dscore = (prob * (dprob - delta)).astype(BF16)
        query_term = nn_dot(keys_across[:, :reach], dscore) * SCALE
        for g in range(GROUP):
            query_grad_ref[span, g * HD : (g + 1) * HD] = jnp.transpose(
                query_term[:, g * HALF : (g + 1) * HALF]
            ).astype(BF16)
        key_term = nn_dot(dscore[front_len:], query)
        value_term = nn_dot(prob[front_len:].astype(BF16), grad)
        if key_total is None:
            key_total, value_total = key_term, value_term
        else:
            done = key_total.shape[0]
            key_total = jnp.concatenate(
                [key_total + key_term[:done], key_term[done:]], axis=0
            )
            value_total = jnp.concatenate(
                [value_total + value_term[:done], value_term[done:]], axis=0
            )
    key_grad_ref[...] = (key_total * SCALE).astype(BF16)
    value_grad_ref[...] = value_total.astype(BF16)


def attention_specs(rows, shards_n, both):
    wide = pl.BlockSpec((rows, GROUP * HD), lambda k: (0, k))
    narrow = pl.BlockSpec((rows, HD), lambda k: (0, k))
    front = pl.BlockSpec((shards_n, both, HD), lambda k: (0, 0, k))
    stats = pl.BlockSpec(
        (None, rows // HALF, 8, GROUP * HALF), lambda k: (k, 0, 0, 0)
    )
    return wide, narrow, front, stats


def params(mib):
    return pltpu.CompilerParams(vmem_limit_bytes=mib * 1024 * 1024)


def cost(matmuls, keys):
    flops = 2 * KVH * GROUP * 256 * keys * HD * matmuls
    return pl.CostEstimate(
        flops=flops, bytes_accessed=3 << 20, transcendentals=KVH * GROUP * 256 * keys
    )


def own_stats(length, query, grad, keys, values, group, copies):
    rows = query.shape[0]
    slots = [m * CORES + core for core in range(CORES) for m in FULL_ORDER]
    slots = np.repeat(np.array(slots, np.int32), copies)[None]
    return pl.pallas_call(
        own_kernel,
        out_shape=(
            jax.ShapeDtypeStruct((KVH, rows // HALF, 8, GROUP * HALF), F32),
            jax.ShapeDtypeStruct(slots.shape, jnp.int32),
        ),
        in_specs=[SMEM] + [VMEM] * 6,
        out_specs=(VMEM, VMEM),
        compiler_params=params(16),
        cost_estimate=cost(2, 256),
    )(length, query, grad, keys, values, group[None], slots)


def front_part(length, query, grad, front, own):
    shards_n, both, _ = front.shape
    return pl.pallas_call(
        front_kernel,
        out_shape=(
            jax.ShapeDtypeStruct((shards_n, KVH, both, HD), BF16),
            jax.ShapeDtypeStruct(own.shape, F32),
        ),
        in_specs=[SMEM, VMEM, VMEM, VMEM, VMEM],
        out_specs=(HBM, VMEM),
        scratch_shapes=[
            pltpu.VMEM((KVH, shards_n, both, HD), BF16),
            pltpu.SemaphoreType.DMA((KVH,)),
        ],
        compiler_params=params(16),
        cost_estimate=cost(4, 128),
    )(length, query, grad, front, own)


def rest_part(length, query, grad, keys, values, front, full):
    shards_n, both, _ = front.shape
    wide, narrow, front_spec, stats = attention_specs(query.shape[0], shards_n, both)
    return pl.pallas_call(
        rest_kernel,
        grid=(KVH,),
        out_shape=(
            jax.ShapeDtypeStruct(query.shape, BF16),
            jax.ShapeDtypeStruct(keys.shape, BF16),
            jax.ShapeDtypeStruct(values.shape, BF16),
            jax.ShapeDtypeStruct((8, HD), F32),
        ),
        in_specs=[SMEM, wide, wide, narrow, narrow, front_spec, stats],
        out_specs=(wide, narrow, narrow, pl.BlockSpec((8, HD), lambda k: (0, 0))),
        compiler_params=params(24),
        cost_estimate=cost(5, 384),
    )(length, query, grad, keys, values, front, full)


def add_kernel(num_prompts, owners_ref, terms_ref, _, out_ref):
    count = terms_ref.shape[0]
    total = out_ref.shape[1]
    rows = total // num_prompts
    row_ids = lax.broadcasted_iota(jnp.int32, (total, count), 0)
    col_ids = lax.broadcasted_iota(jnp.int32, (total, count), 1)
    hit = (owners_ref[...] == row_ids // rows) & (row_ids % rows == col_ids % rows)
    sums = nn_dot(jnp.where(hit, 1.0, 0.0).astype(BF16), terms_ref[...]).astype(BF16)
    out_ref[...] = jnp.broadcast_to(sums[None], out_ref.shape)


def add_by_prompt(owners, terms, after, num_prompts, rows, copies):
    return pl.pallas_call(
        functools.partial(add_kernel, num_prompts),
        out_shape=jax.ShapeDtypeStruct((copies, rows * num_prompts, HD), BF16),
        in_specs=[VMEM, VMEM, VMEM],
        out_specs=VMEM,
        compiler_params=params(4),
    )(owners, terms, after)


def place_kernel(parts_ref, key_hbm, value_hbm, out_ref, sems):
    came = [NEAR_ORDER.index(chip) for chip in CHIP_ORDER]
    _, prompts, own, _ = out_ref.shape
    blocks = parts_ref.shape[0] // (2 * KVH)
    rows = own // blocks
    size = prompts * own
    to = lax.broadcasted_iota(jnp.int32, (size, size), 0)
    at = lax.broadcasted_iota(jnp.int32, (size, size), 1)
    prompt, row = to // own, to % own
    hit = at == (row // rows) * (rows * prompts) + prompt * rows + row % rows
    move = jnp.where(hit, 1.0, 0.0).astype(BF16)
    copies = []
    for side, out_hbm in enumerate((key_hbm, value_hbm)):
        for k in range(KVH):
            first = (k * 2 + side) * blocks
            block = jnp.concatenate(
                [parts_ref[came[first + w]] for w in range(blocks)], axis=0
            )
            out_ref[side, :, :, k * HD : (k + 1) * HD] = nn_dot(move, block).reshape(
                prompts, own, HD
            )
        copies.append(pltpu.make_async_copy(out_ref.at[side], out_hbm, sems.at[side]))
        copies[-1].start()
    for copy in copies:
        copy.wait()


def place(parts, shape):
    return pl.pallas_call(
        place_kernel,
        out_shape=(jax.ShapeDtypeStruct(shape, F32), jax.ShapeDtypeStruct(shape, F32)),
        in_specs=[VMEM],
        out_specs=(HBM, HBM),
        scratch_shapes=[
            pltpu.VMEM((2,) + shape, F32),
            pltpu.SemaphoreType.DMA((2,)),
        ],
        compiler_params=params(4),
    )(parts)


def exchange(blocks, axes, groups):
    return lax.all_to_all(blocks, axes, 0, 0, axis_index_groups=groups)


def shards(query, resp_keys, resp_values, prompt_keys, prompt_values, out_grad, group, lengths):
    places, chips = lax.axis_size("prompt"), lax.axis_size("chip")
    num_prompts, own, width = prompt_keys.shape
    wanted = pick(group, prompt_keys, prompt_values, places)
    front = exchange(wanted, ("prompt", "chip"), front_groups())
    query, grad, keys, values = query[0], out_grad[0], resp_keys[0], resp_values[0]
    rows = 2 * own * width // (chips * HD)
    stats, owners = own_stats(lengths, query, grad, keys, values, group, rows)
    front_grad, full = front_part(lengths, query, grad, front, stats)
    terms = exchange(
        front_grad.reshape(places * chips, rows, HD), ("prompt", "chip"), [FULL_ORDER]
    )
    query_grad, key_grad, value_grad, done = rest_part(
        lengths, query, grad, keys, values, front, full
    )
    terms = lax.all_gather(terms, "core", axis=0).reshape(-1, HD)
    sums = add_by_prompt(owners, terms, done, num_prompts, rows, chips)
    parts = exchange(sums, "chip", [NEAR_ORDER])
    prompt_key_grad, prompt_value_grad = place(parts, prompt_keys.shape)
    return (
        query_grad[None],
        key_grad[None],
        value_grad[None],
        prompt_key_grad,
        prompt_value_grad,
    )


def solution(mesh):
    places, resps = mesh.devices.shape
    mesh = Mesh(
        mesh.devices.reshape(places, resps // CORES, CORES), ("prompt", "chip", "core")
    )
    every = ("prompt", "chip", "core")
    row = P(every, None, None)
    front = P(None, "prompt", None)
    return jax.shard_map(
        shards,
        mesh=mesh,
        in_specs=(row, row, row, front, front, row, P(), P(every)),
        out_specs=(row, row, row, front, front),
        check_vma=False,
    )
```

```python
import functools
import math

import jax
import jax.numpy as jnp
import numpy as np
from jax import lax
from jax.experimental import pallas as pl
from jax.experimental.pallas import tpu as pltpu
from jax.sharding import Mesh
from jax.sharding import PartitionSpec as P

HD = 128
KVH = 4
GROUP = 4
CORES = 2
HALF = 128
SCALE = 1.0 / math.sqrt(HD)
LOG2E = math.log2(math.e)
PLACES = (4, 4)
CHIPS = (2, 8)
LATE_PLACE = (2, 2)
LATE_CHIP = (0, 4)
BF16 = jnp.bfloat16
F32 = jnp.float32
SMEM = pl.BlockSpec(memory_space=pltpu.SMEM)
VMEM = pl.BlockSpec(memory_space=pltpu.VMEM)
HBM = pl.BlockSpec(memory_space=pltpu.HBM)


def ring(a, b, size):
    return min((a - b) % size, (b - a) % size)


def hops(a, b, sizes, steps):
    return sum(ring(i, j, n) * step for i, j, n, step in zip(a, b, sizes, steps))


def far_first(sizes, steps, root):
    members = [(i, j) for i in range(sizes[0]) for j in range(sizes[1])]
    members.sort(key=lambda m: (m != root, -hops(m, root, sizes, steps)))
    return [i * sizes[1] + j for i, j in members]


PLACE_ORDER = far_first(PLACES, (1, 2), LATE_PLACE)
ROW_ORDER = far_first((1, CHIPS[1]), (1, 1), (0, LATE_CHIP[1]))
NEAR_ORDER = [row ^ LATE_CHIP[1] for row in range(CHIPS[1])]
CHIP_COUNT = CHIPS[0] * CHIPS[1]


def nt_dot(a, b):
    return lax.dot_general(a, b, (((1,), (1,)), ((), ())), preferred_element_type=F32)


def nn_dot(a, b):
    return lax.dot_general(a, b, (((1,), (0,)), ((), ())), preferred_element_type=F32)


def exp_scaled(x):
    return jnp.exp2(x * (SCALE * LOG2E))


def stack_heads(block, half, k=0):
    span = slice(half * HALF, (half + 1) * HALF)
    return jnp.concatenate(
        [block[span, h * HD : (h + 1) * HD] for h in range(k * GROUP, (k + 1) * GROUP)],
        axis=0,
    )


def live_grad(grad_ref, length, half, k=0):
    grad = stack_heads(grad_ref, half, k)
    row_ids = lax.broadcasted_iota(jnp.int32, grad.shape, 0) % HALF
    return jnp.where(row_ids + half * HALF < length, grad, jnp.zeros_like(grad))


def causal(scores):
    reach, wide = scores.shape
    key_ids = lax.broadcasted_iota(jnp.int32, (HALF, wide), 0)
    row_ids = lax.broadcasted_iota(jnp.int32, (HALF, wide), 1) % HALF
    last = jnp.where(key_ids <= row_ids, scores[reach - HALF :], -1e30)
    if reach == HALF:
        return last
    return jnp.concatenate([scores[: reach - HALF], last], axis=0)


def front_parts(front_ref, k=0):
    shards_n, both, _ = front_ref.shape
    front = front_ref[:, :, k * HD : (k + 1) * HD].astype(F32)
    keys, values = front[:, : both // 2], front[:, both // 2 :]
    return (
        keys.reshape(shards_n * both // 2, HD).astype(BF16),
        values.reshape(shards_n * both // 2, HD).astype(BF16),
    )


def peer_chip(side, row, place):
    bent = place % PLACES[1] >= PLACES[1] // 2
    return (1 - side if bent else side) * CHIPS[1] + row


def sum_groups():
    return [
        [
            place * CHIP_COUNT + peer_chip(side, row, place)
            for place in PLACE_ORDER
            for row in ROW_ORDER
        ]
        for side in range(CHIPS[0])
    ]


def own_side(chip):
    bent = lax.axis_index("prompt") % PLACES[1] >= PLACES[1] // 2
    return jnp.where(bent, 1 - chip // CHIPS[1], chip // CHIPS[1])


def front_groups():
    return [
        [place * CHIP_COUNT + peer_chip(side, row, place) for place in PLACE_ORDER]
        for side in range(CHIPS[0])
        for row in range(CHIPS[1])
    ]


def pick_kernel(
    group_hbm, keys_hbm, values_hbm, out_ref, group_ref, keys_ref, values_ref, sems
):
    copies = [
        pltpu.make_async_copy(source, target, sems.at[i])
        for i, (source, target) in enumerate(
            zip((group_hbm, keys_hbm, values_hbm), (group_ref, keys_ref, values_ref))
        )
    ]
    for copy in copies:
        copy.start()
    chip, core = lax.axis_index("chip"), lax.axis_index("core")
    row = chip % CHIPS[1]
    side = own_side(chip)
    for copy in copies:
        copy.wait()
    for i, place in enumerate(PLACE_ORDER):
        peer = place * CHIP_COUNT + peer_chip(side, row, place)
        owner = group_ref[peer * CORES + core]
        both = jnp.concatenate(
            [keys_ref[owner].astype(F32), values_ref[owner].astype(F32)], axis=0
        )
        out_ref[i] = both.astype(BF16)


def pick(group, keys, values, count):
    _, rows, width = keys.shape
    return pl.pallas_call(
        pick_kernel,
        out_shape=jax.ShapeDtypeStruct((count, 2 * rows, width), BF16),
        in_specs=[HBM] * 3,
        out_specs=VMEM,
        scratch_shapes=[
            pltpu.SMEM(group.shape, group.dtype),
            pltpu.VMEM(keys.shape, keys.dtype),
            pltpu.VMEM(values.shape, values.dtype),
            pltpu.SemaphoreType.DMA((3,)),
        ],
        compiler_params=params(56),
    )(group, keys, values)


def own_kernel(
    length_ref,
    query_ref,
    grad_ref,
    keys_ref,
    values_ref,
    group_ref,
    slots_ref,
    stats_ref,
    owners_ref,
):
    length = length_ref[0]
    for k in range(KVH):
        features = slice(k * HD, (k + 1) * HD)
        for half in range(query_ref.shape[0] // HALF):
            reach = (half + 1) * HALF
            query = stack_heads(query_ref, half, k)
            grad = live_grad(grad_ref, length, half, k)
            scores = causal(nt_dot(keys_ref[:reach, features], query))
            top = jnp.max(scores, axis=0, keepdims=True)
            weights = exp_scaled(scores - top)
            dprob = nt_dot(values_ref[:reach, features], grad)
            total = jnp.sum(weights, axis=0, keepdims=True)
            dot = jnp.sum(weights * dprob, axis=0, keepdims=True)
            fill = jnp.zeros((5, top.shape[1]), F32)
            stats_ref[k, half] = jnp.concatenate([top, total, dot, fill], axis=0)
    count, size = group_ref.shape[1], slots_ref.shape[1]
    side = own_side(lax.axis_index("chip"))
    slots = jnp.where(side == 0, slots_ref[0:1], slots_ref[1:2])
    slots = slots + lax.axis_index("core")
    hit = lax.broadcasted_iota(jnp.int32, (count, size), 0) == slots
    group = jnp.broadcast_to(group_ref[...].astype(F32).astype(BF16), (8, count))
    owners = nn_dot(group, jnp.where(hit, 1.0, 0.0).astype(BF16))
    owners_ref[...] = owners[:1].astype(jnp.int32)


def front_kernel(
    length_ref,
    query_ref,
    grad_ref,
    front_ref,
    stats_ref,
    front_grad_hbm,
    full_ref,
    front_grad_ref,
    sems,
):
    length = length_ref[0]
    _, shards_n, both, _ = front_grad_ref.shape
    copies = [
        pltpu.make_async_copy(front_grad_ref.at[k], front_grad_hbm.at[:, k], sems.at[k])
        for k in range(KVH)
    ]
    front_len = shards_n * (both // 2)
    halves = range(query_ref.shape[0] // HALF)

    def begin(k):
        keys, values = front_parts(front_ref, k)
        query = jnp.concatenate([stack_heads(query_ref, half, k) for half in halves])
        grad = jnp.concatenate(
            [live_grad(grad_ref, length, half, k) for half in halves]
        )
        both = jnp.concatenate([query, grad], axis=1)
        none = jnp.zeros_like(keys)
        front = jnp.concatenate(
            [
                jnp.concatenate([keys, none], axis=1),
                jnp.concatenate([none, values], axis=1),
            ]
        )
        return both, nt_dot(front, both)

    ahead = begin(0)
    for k in range(KVH):
        rows, dots = ahead
        if k + 1 < KVH:
            ahead = begin(k + 1)
        scores, dprob = dots[:front_len], dots[front_len:]
        stats = jnp.concatenate([stats_ref[k, half] for half in halves], axis=1)
        own_top, own_total, own_dot = stats[0:1], stats[1:2], stats[2:3]
        top = jnp.maximum(jnp.max(scores, axis=0, keepdims=True), own_top)
        weights = exp_scaled(scores - top)
        rescale = exp_scaled(own_top - top)
        total = jnp.sum(weights, axis=0, keepdims=True) + own_total * rescale
        inverse = 1.0 / total
        prob = weights * inverse
        dots = jnp.sum(weights * dprob, axis=0, keepdims=True) + own_dot * rescale
        delta = dots * inverse
        dscore = (prob * (dprob - delta)).astype(BF16)
        sums = nn_dot(jnp.concatenate([dscore, prob.astype(BF16)]), rows)
        key_total = sums[:front_len, :HD] * SCALE
        value_total = sums[front_len:, HD:]
        fill = jnp.zeros((5, top.shape[1]), F32)
        full = jnp.concatenate([top, inverse, delta, fill], axis=0)
        for half in halves:
            full_ref[k, half] = full[:, half * GROUP * HALF : (half + 1) * GROUP * HALF]
        front_grad_ref[k] = jnp.concatenate(
            [
                key_total.reshape(shards_n, both // 2, HD),
                value_total.reshape(shards_n, both // 2, HD),
            ],
            axis=1,
        ).astype(BF16)
        copies[k].start()
    for copy in copies:
        copy.wait()


def rest_kernel(
    length_ref,
    query_ref,
    grad_ref,
    keys_ref,
    values_ref,
    front_ref,
    full_ref,
    query_grad_ref,
    key_grad_ref,
    value_grad_ref,
    done_ref,
):
    done_ref[...] = jnp.zeros_like(done_ref)
    length = length_ref[0]
    front_keys, front_values = front_parts(front_ref)
    front_len = front_keys.shape[0]
    all_keys = jnp.concatenate([front_keys, keys_ref[...]], axis=0)
    all_values = jnp.concatenate([front_values, values_ref[...]], axis=0)
    keys_across = jnp.transpose(all_keys)
    key_total, value_total = None, None
    for half in range(query_ref.shape[0] // HALF):
        reach = front_len + (half + 1) * HALF
        span = slice(half * HALF, (half + 1) * HALF)
        query = stack_heads(query_ref, half)
        grad = live_grad(grad_ref, length, half)
        full = full_ref[half]
        top, inverse, delta = full[0:1], full[1:2], full[2:3]
        scores = causal(nt_dot(all_keys[:reach], query))
        prob = exp_scaled(scores - top) * inverse
        dprob = nt_dot(all_values[:reach], grad)
        dscore = (prob * (dprob - delta)).astype(BF16)
        query_term = nn_dot(keys_across[:, :reach], dscore) * SCALE
        for g in range(GROUP):
            query_grad_ref[span, g * HD : (g + 1) * HD] = jnp.transpose(
                query_term[:, g * HALF : (g + 1) * HALF]
            ).astype(BF16)
        key_term = nn_dot(dscore[front_len:], query)
        value_term = nn_dot(prob[front_len:].astype(BF16), grad)
        if key_total is None:
            key_total, value_total = key_term, value_term
        else:
            done = key_total.shape[0]
            key_total = jnp.concatenate(
                [key_total + key_term[:done], key_term[done:]], axis=0
            )
            value_total = jnp.concatenate(
                [value_total + value_term[:done], value_term[done:]], axis=0
            )
    key_grad_ref[...] = (key_total * SCALE).astype(BF16)
    value_grad_ref[...] = value_total.astype(BF16)


def attention_specs(rows, shards_n, both):
    wide = pl.BlockSpec((rows, GROUP * HD), lambda k: (0, k))
    narrow = pl.BlockSpec((rows, HD), lambda k: (0, k))
    front = pl.BlockSpec((shards_n, both, HD), lambda k: (0, 0, k))
    stats = pl.BlockSpec(
        (None, rows // HALF, 8, GROUP * HALF), lambda k: (k, 0, 0, 0)
    )
    return wide, narrow, front, stats


def params(mib):
    return pltpu.CompilerParams(vmem_limit_bytes=mib * 1024 * 1024)


def cost(matmuls, keys):
    flops = 2 * KVH * GROUP * 256 * keys * HD * matmuls
    return pl.CostEstimate(
        flops=flops, bytes_accessed=3 << 20, transcendentals=KVH * GROUP * 256 * keys
    )


def own_stats(length, query, grad, keys, values, group, copies):
    rows = query.shape[0]
    slots = np.repeat(np.array(sum_groups(), np.int32) * CORES, copies, axis=1)
    return pl.pallas_call(
        own_kernel,
        out_shape=(
            jax.ShapeDtypeStruct((KVH, rows // HALF, 8, GROUP * HALF), F32),
            jax.ShapeDtypeStruct((1, slots.shape[1]), jnp.int32),
        ),
        in_specs=[SMEM] + [VMEM] * 6,
        out_specs=(VMEM, VMEM),
        compiler_params=params(16),
        cost_estimate=cost(2, 256),
    )(length, query, grad, keys, values, group[None], slots)


def front_part(length, query, grad, front, own):
    shards_n, both, _ = front.shape
    return pl.pallas_call(
        front_kernel,
        out_shape=(
            jax.ShapeDtypeStruct((shards_n, KVH, both, HD), BF16),
            jax.ShapeDtypeStruct(own.shape, F32),
        ),
        in_specs=[SMEM, VMEM, VMEM, VMEM, VMEM],
        out_specs=(HBM, VMEM),
        scratch_shapes=[
            pltpu.VMEM((KVH, shards_n, both, HD), BF16),
            pltpu.SemaphoreType.DMA((KVH,)),
        ],
        compiler_params=params(16),
        cost_estimate=cost(4, 128),
    )(length, query, grad, front, own)


def rest_part(length, query, grad, keys, values, front, full):
    shards_n, both, _ = front.shape
    wide, narrow, front_spec, stats = attention_specs(query.shape[0], shards_n, both)
    return pl.pallas_call(
        rest_kernel,
        grid=(KVH,),
        out_shape=(
            jax.ShapeDtypeStruct(query.shape, BF16),
            jax.ShapeDtypeStruct(keys.shape, BF16),
            jax.ShapeDtypeStruct(values.shape, BF16),
            jax.ShapeDtypeStruct((8, HD), F32),
        ),
        in_specs=[SMEM, wide, wide, narrow, narrow, front_spec, stats],
        out_specs=(wide, narrow, narrow, pl.BlockSpec((8, HD), lambda k: (0, 0))),
        compiler_params=params(24),
        cost_estimate=cost(5, 384),
    )(length, query, grad, keys, values, front, full)


def add_kernel(num_prompts, owners_ref, terms_ref, _, out_ref):
    count = terms_ref.shape[0]
    total = out_ref.shape[0]
    rows = total // num_prompts
    row_ids = lax.broadcasted_iota(jnp.int32, (total, count), 0)
    col_ids = lax.broadcasted_iota(jnp.int32, (total, count), 1)
    hit = (owners_ref[...] == row_ids // rows) & (row_ids % rows == col_ids % rows)
    hit = jnp.where(hit, 1.0, 0.0).astype(BF16)
    out_ref[...] = nn_dot(hit, terms_ref[...]).astype(BF16)


def add_by_prompt(owners, terms, after, num_prompts, rows):
    return pl.pallas_call(
        functools.partial(add_kernel, num_prompts),
        out_shape=jax.ShapeDtypeStruct((rows * num_prompts, HD), BF16),
        in_specs=[VMEM, VMEM, VMEM],
        out_specs=VMEM,
        compiler_params=params(4),
    )(owners, terms, after)


def spread_kernel(sums_ref, out_ref):
    total = jnp.sum(sums_ref[...].astype(F32), axis=0).astype(BF16)
    out_ref[...] = jnp.broadcast_to(total[None], out_ref.shape)


def spread(sums, copies):
    return pl.pallas_call(
        spread_kernel,
        out_shape=jax.ShapeDtypeStruct((copies,) + sums.shape[1:], BF16),
        in_specs=[VMEM],
        out_specs=VMEM,
        compiler_params=params(4),
    )(sums)


def place_kernel(parts_ref, key_hbm, value_hbm, out_ref, sems):
    _, prompts, own, _ = out_ref.shape
    came = [NEAR_ORDER.index(row) for row in ROW_ORDER]
    copies = []
    for side, out_hbm in enumerate((key_hbm, value_hbm)):
        for k in range(KVH):
            block = parts_ref[came[k * 2 + side]].astype(F32)
            out_ref[side, :, :, k * HD : (k + 1) * HD] = block.reshape(prompts, own, HD)
        copies.append(pltpu.make_async_copy(out_ref.at[side], out_hbm, sems.at[side]))
        copies[-1].start()
    for copy in copies:
        copy.wait()


def place(parts, shape):
    return pl.pallas_call(
        place_kernel,
        out_shape=(jax.ShapeDtypeStruct(shape, F32), jax.ShapeDtypeStruct(shape, F32)),
        in_specs=[VMEM],
        out_specs=(HBM, HBM),
        scratch_shapes=[
            pltpu.VMEM((2,) + shape, F32),
            pltpu.SemaphoreType.DMA((2,)),
        ],
        compiler_params=params(4),
    )(parts)


def exchange(blocks, axes, groups):
    return lax.all_to_all(blocks, axes, 0, 0, axis_index_groups=groups)


def shards(query, resp_keys, resp_values, prompt_keys, prompt_values, out_grad, group, lengths):
    places = lax.axis_size("prompt")
    num_prompts, own, _ = prompt_keys.shape
    wanted = pick(group, prompt_keys, prompt_values, places)
    front = exchange(wanted, ("prompt", "chip"), front_groups())
    query, grad, keys, values = query[0], out_grad[0], resp_keys[0], resp_values[0]
    rows = own
    stats, owners = own_stats(lengths, query, grad, keys, values, group, rows)
    front_grad, full = front_part(lengths, query, grad, front, stats)
    terms = exchange(
        front_grad.reshape(-1, rows, HD), ("prompt", "chip"), sum_groups()
    )
    query_grad, key_grad, value_grad, done = rest_part(
        lengths, query, grad, keys, values, front, full
    )
    sums = add_by_prompt(owners, terms.reshape(-1, HD), done, num_prompts, rows)
    near = [
        [(z * CHIPS[1] + row) * CORES + core for z in range(CHIPS[0]) for core in range(CORES)]
        for row in range(CHIPS[1])
    ]
    sums = lax.all_gather(sums, ("chip", "core"), axis=0, axis_index_groups=near)
    along = [[z * CHIPS[1] + row for row in NEAR_ORDER] for z in range(CHIPS[0])]
    parts = exchange(spread(sums, CHIPS[1]), "chip", along)
    prompt_key_grad, prompt_value_grad = place(parts, prompt_keys.shape)
    return (
        query_grad[None],
        key_grad[None],
        value_grad[None],
        prompt_key_grad,
        prompt_value_grad,
    )


def solution(mesh):
    places, resps = mesh.devices.shape
    mesh = Mesh(
        mesh.devices.reshape(places, resps // CORES, CORES), ("prompt", "chip", "core")
    )
    every = ("prompt", "chip", "core")
    row = P(every, None, None)
    front = P(None, "prompt", None)
    return jax.shard_map(
        shards,
        mesh=mesh,
        in_specs=(row, row, row, front, front, row, P(), P(every)),
        out_specs=(row, row, row, front, front),
        check_vma=False,
    )
```

```python
import functools
import math

import jax
import jax.numpy as jnp
import numpy as np
from jax import lax
from jax.experimental import pallas as pl
from jax.experimental.pallas import tpu as pltpu
from jax.sharding import Mesh
from jax.sharding import PartitionSpec as P

HD = 128
KVH = 4
GROUP = 4
CORES = 2
HALF = 128
SCALE = 1.0 / math.sqrt(HD)
LOG2E = math.log2(math.e)
PLACES = (4, 4)
CHIPS = (2, 8)
LATE_PLACE = (2, 2)
LATE_CHIP = (0, 4)
BF16 = jnp.bfloat16
F32 = jnp.float32
SMEM = pl.BlockSpec(memory_space=pltpu.SMEM)
VMEM = pl.BlockSpec(memory_space=pltpu.VMEM)
HBM = pl.BlockSpec(memory_space=pltpu.HBM)


def ring(a, b, size):
    return min((a - b) % size, (b - a) % size)


def hops(a, b, sizes, steps):
    return sum(ring(i, j, n) * step for i, j, n, step in zip(a, b, sizes, steps))


def far_first(sizes, steps, root):
    members = [(i, j) for i in range(sizes[0]) for j in range(sizes[1])]
    members.sort(key=lambda m: (m != root, -hops(m, root, sizes, steps)))
    return [i * sizes[1] + j for i, j in members]


PLACE_ORDER = far_first(PLACES, (1, 2), LATE_PLACE)
CHIP_ORDER = far_first(CHIPS, (1, 1), LATE_CHIP)
NEAR_ORDER = [c ^ CHIP_ORDER[0] for c in range(len(CHIP_ORDER))]
FULL_ORDER = [p * len(CHIP_ORDER) + c for p in PLACE_ORDER for c in CHIP_ORDER]


def nt_dot(a, b):
    return lax.dot_general(a, b, (((1,), (1,)), ((), ())), preferred_element_type=F32)


def nn_dot(a, b):
    return lax.dot_general(a, b, (((1,), (0,)), ((), ())), preferred_element_type=F32)


def exp_scaled(x):
    return jnp.exp2(x * (SCALE * LOG2E))


def stack_heads(block, half, k=0):
    span = slice(half * HALF, (half + 1) * HALF)
    return jnp.concatenate(
        [block[span, h * HD : (h + 1) * HD] for h in range(k * GROUP, (k + 1) * GROUP)],
        axis=0,
    )


def live_grad(grad_ref, length, half, k=0):
    grad = stack_heads(grad_ref, half, k)
    row_ids = lax.broadcasted_iota(jnp.int32, grad.shape, 0) % HALF
    return jnp.where(row_ids + half * HALF < length, grad, jnp.zeros_like(grad))


def causal(scores):
    reach, wide = scores.shape
    key_ids = lax.broadcasted_iota(jnp.int32, (HALF, wide), 0)
    row_ids = lax.broadcasted_iota(jnp.int32, (HALF, wide), 1) % HALF
    last = jnp.where(key_ids <= row_ids, scores[reach - HALF :], -1e30)
    if reach == HALF:
        return last
    return jnp.concatenate([scores[: reach - HALF], last], axis=0)


def front_parts(front_ref, k=0):
    shards_n, both, _ = front_ref.shape
    front = front_ref[:, :, k * HD : (k + 1) * HD].astype(F32)
    keys, values = front[:, : both // 2], front[:, both // 2 :]
    return (
        keys.reshape(shards_n * both // 2, HD).astype(BF16),
        values.reshape(shards_n * both // 2, HD).astype(BF16),
    )


def peer_chip(side, row, place):
    bent = place % PLACES[1] >= PLACES[1] // 2
    return (1 - side if bent else side) * CHIPS[1] + row


def front_groups():
    return [
        [place * len(CHIP_ORDER) + peer_chip(side, row, place) for place in PLACE_ORDER]
        for side in range(CHIPS[0])
        for row in range(CHIPS[1])
    ]


def pick_kernel(
    group_hbm, keys_hbm, values_hbm, out_ref, group_ref, keys_ref, values_ref, sems
):
    copies = [
        pltpu.make_async_copy(source, target, sems.at[i])
        for i, (source, target) in enumerate(
            zip((group_hbm, keys_hbm, values_hbm), (group_ref, keys_ref, values_ref))
        )
    ]
    for copy in copies:
        copy.start()
    chip, core = lax.axis_index("chip"), lax.axis_index("core")
    row = chip % CHIPS[1]
    bent = lax.axis_index("prompt") % PLACES[1] >= PLACES[1] // 2
    side = jnp.where(bent, 1 - chip // CHIPS[1], chip // CHIPS[1])
    for copy in copies:
        copy.wait()
    for i, place in enumerate(PLACE_ORDER):
        peer = place * len(CHIP_ORDER) + peer_chip(side, row, place)
        owner = group_ref[peer * CORES + core]
        both = jnp.concatenate(
            [keys_ref[owner].astype(F32), values_ref[owner].astype(F32)], axis=0
        )
        out_ref[i] = both.astype(BF16)


def pick(group, keys, values, count):
    _, rows, width = keys.shape
    return pl.pallas_call(
        pick_kernel,
        out_shape=jax.ShapeDtypeStruct((count, 2 * rows, width), BF16),
        in_specs=[HBM] * 3,
        out_specs=VMEM,
        scratch_shapes=[
            pltpu.SMEM(group.shape, group.dtype),
            pltpu.VMEM(keys.shape, keys.dtype),
            pltpu.VMEM(values.shape, values.dtype),
            pltpu.SemaphoreType.DMA((3,)),
        ],
        compiler_params=params(56),
    )(group, keys, values)


def own_kernel(
    length_ref,
    query_ref,
    grad_ref,
    keys_ref,
    values_ref,
    group_ref,
    slots_ref,
    stats_ref,
    owners_ref,
):
    length = length_ref[0]
    for k in range(KVH):
        features = slice(k * HD, (k + 1) * HD)
        for half in range(query_ref.shape[0] // HALF):
            reach = (half + 1) * HALF
            query = stack_heads(query_ref, half, k)
            grad = live_grad(grad_ref, length, half, k)
            scores = causal(nt_dot(keys_ref[:reach, features], query))
            top = jnp.max(scores, axis=0, keepdims=True)
            weights = exp_scaled(scores - top)
            dprob = nt_dot(values_ref[:reach, features], grad)
            total = jnp.sum(weights, axis=0, keepdims=True)
            dot = jnp.sum(weights * dprob, axis=0, keepdims=True)
            fill = jnp.zeros((5, top.shape[1]), F32)
            stats_ref[k, half] = jnp.concatenate([top, total, dot, fill], axis=0)
    count, size = group_ref.shape[1], slots_ref.shape[1]
    hit = lax.broadcasted_iota(jnp.int32, (count, size), 0) == slots_ref[...]
    group = jnp.broadcast_to(group_ref[...].astype(F32).astype(BF16), (8, count))
    owners = nn_dot(group, jnp.where(hit, 1.0, 0.0).astype(BF16))
    owners_ref[...] = owners[:1].astype(jnp.int32)


def front_kernel(
    length_ref,
    query_ref,
    grad_ref,
    front_ref,
    stats_ref,
    front_grad_hbm,
    full_ref,
    front_grad_ref,
    sems,
):
    length = length_ref[0]
    _, shards_n, both, _ = front_grad_ref.shape
    copies = [
        pltpu.make_async_copy(front_grad_ref.at[k], front_grad_hbm.at[:, k], sems.at[k])
        for k in range(KVH)
    ]
    front_len = shards_n * (both // 2)
    halves = range(query_ref.shape[0] // HALF)

    def begin(k):
        keys, values = front_parts(front_ref, k)
        query = jnp.concatenate([stack_heads(query_ref, half, k) for half in halves])
        grad = jnp.concatenate(
            [live_grad(grad_ref, length, half, k) for half in halves]
        )
        both = jnp.concatenate([query, grad], axis=1)
        none = jnp.zeros_like(keys)
        front = jnp.concatenate(
            [
                jnp.concatenate([keys, none], axis=1),
                jnp.concatenate([none, values], axis=1),
            ]
        )
        return both, nt_dot(front, both)

    ahead = begin(0)
    for k in range(KVH):
        rows, dots = ahead
        if k + 1 < KVH:
            ahead = begin(k + 1)
        scores, dprob = dots[:front_len], dots[front_len:]
        stats = jnp.concatenate([stats_ref[k, half] for half in halves], axis=1)
        own_top, own_total, own_dot = stats[0:1], stats[1:2], stats[2:3]
        top = jnp.maximum(jnp.max(scores, axis=0, keepdims=True), own_top)
        weights = exp_scaled(scores - top)
        rescale = exp_scaled(own_top - top)
        total = jnp.sum(weights, axis=0, keepdims=True) + own_total * rescale
        inverse = 1.0 / total
        prob = weights * inverse
        dots = jnp.sum(weights * dprob, axis=0, keepdims=True) + own_dot * rescale
        delta = dots * inverse
        dscore = (prob * (dprob - delta)).astype(BF16)
        sums = nn_dot(jnp.concatenate([dscore, prob.astype(BF16)]), rows)
        key_total = sums[:front_len, :HD] * SCALE
        value_total = sums[front_len:, HD:]
        fill = jnp.zeros((5, top.shape[1]), F32)
        full = jnp.concatenate([top, inverse, delta, fill], axis=0)
        for half in halves:
            full_ref[k, half] = full[:, half * GROUP * HALF : (half + 1) * GROUP * HALF]
        front_grad_ref[k] = jnp.concatenate(
            [
                key_total.reshape(shards_n, both // 2, HD),
                value_total.reshape(shards_n, both // 2, HD),
            ],
            axis=1,
        ).astype(BF16)
        copies[k].start()
    for copy in copies:
        copy.wait()


def rest_kernel(
    length_ref,
    query_ref,
    grad_ref,
    keys_ref,
    values_ref,
    front_ref,
    full_ref,
    query_grad_ref,
    key_grad_ref,
    value_grad_ref,
    done_ref,
):
    done_ref[...] = jnp.zeros_like(done_ref)
    length = length_ref[0]
    front_keys, front_values = front_parts(front_ref)
    front_len = front_keys.shape[0]
    all_keys = jnp.concatenate([front_keys, keys_ref[...]], axis=0)
    all_values = jnp.concatenate([front_values, values_ref[...]], axis=0)
    keys_across = jnp.transpose(all_keys)
    key_total, value_total = None, None
    for half in range(query_ref.shape[0] // HALF):
        reach = front_len + (half + 1) * HALF
        span = slice(half * HALF, (half + 1) * HALF)
        query = stack_heads(query_ref, half)
        grad = live_grad(grad_ref, length, half)
        full = full_ref[half]
        top, inverse, delta = full[0:1], full[1:2], full[2:3]
        scores = causal(nt_dot(all_keys[:reach], query))
        prob = exp_scaled(scores - top) * inverse
        dprob = nt_dot(all_values[:reach], grad)
        dscore = (prob * (dprob - delta)).astype(BF16)
        query_term = nn_dot(keys_across[:, :reach], dscore) * SCALE
        for g in range(GROUP):
            query_grad_ref[span, g * HD : (g + 1) * HD] = jnp.transpose(
                query_term[:, g * HALF : (g + 1) * HALF]
            ).astype(BF16)
        key_term = nn_dot(dscore[front_len:], query)
        value_term = nn_dot(prob[front_len:].astype(BF16), grad)
        if key_total is None:
            key_total, value_total = key_term, value_term
        else:
            done = key_total.shape[0]
            key_total = jnp.concatenate(
                [key_total + key_term[:done], key_term[done:]], axis=0
            )
            value_total = jnp.concatenate(
                [value_total + value_term[:done], value_term[done:]], axis=0
            )
    key_grad_ref[...] = (key_total * SCALE).astype(BF16)
    value_grad_ref[...] = value_total.astype(BF16)


def attention_specs(rows, shards_n, both):
    wide = pl.BlockSpec((rows, GROUP * HD), lambda k: (0, k))
    narrow = pl.BlockSpec((rows, HD), lambda k: (0, k))
    front = pl.BlockSpec((shards_n, both, HD), lambda k: (0, 0, k))
    stats = pl.BlockSpec(
        (None, rows // HALF, 8, GROUP * HALF), lambda k: (k, 0, 0, 0)
    )
    return wide, narrow, front, stats


def params(mib):
    return pltpu.CompilerParams(vmem_limit_bytes=mib * 1024 * 1024)


def cost(matmuls, keys):
    flops = 2 * KVH * GROUP * 256 * keys * HD * matmuls
    return pl.CostEstimate(
        flops=flops, bytes_accessed=3 << 20, transcendentals=KVH * GROUP * 256 * keys
    )


def own_stats(length, query, grad, keys, values, group, copies):
    rows = query.shape[0]
    slots = [m * CORES + core for core in range(CORES) for m in FULL_ORDER]
    slots = np.repeat(np.array(slots, np.int32), copies)[None]
    return pl.pallas_call(
        own_kernel,
        out_shape=(
            jax.ShapeDtypeStruct((KVH, rows // HALF, 8, GROUP * HALF), F32),
            jax.ShapeDtypeStruct(slots.shape, jnp.int32),
        ),
        in_specs=[SMEM] + [VMEM] * 6,
        out_specs=(VMEM, VMEM),
        compiler_params=params(16),
        cost_estimate=cost(2, 256),
    )(length, query, grad, keys, values, group[None], slots)


def front_part(length, query, grad, front, own):
    shards_n, both, _ = front.shape
    return pl.pallas_call(
        front_kernel,
        out_shape=(
            jax.ShapeDtypeStruct((shards_n, KVH, both, HD), BF16),
            jax.ShapeDtypeStruct(own.shape, F32),
        ),
        in_specs=[SMEM, VMEM, VMEM, VMEM, VMEM],
        out_specs=(HBM, VMEM),
        scratch_shapes=[
            pltpu.VMEM((KVH, shards_n, both, HD), BF16),
            pltpu.SemaphoreType.DMA((KVH,)),
        ],
        compiler_params=params(16),
        cost_estimate=cost(4, 128),
    )(length, query, grad, front, own)


def rest_part(length, query, grad, keys, values, front, full):
    shards_n, both, _ = front.shape
    wide, narrow, front_spec, stats = attention_specs(query.shape[0], shards_n, both)
    return pl.pallas_call(
        rest_kernel,
        grid=(KVH,),
        out_shape=(
            jax.ShapeDtypeStruct(query.shape, BF16),
            jax.ShapeDtypeStruct(keys.shape, BF16),
            jax.ShapeDtypeStruct(values.shape, BF16),
            jax.ShapeDtypeStruct((8, HD), F32),
        ),
        in_specs=[SMEM, wide, wide, narrow, narrow, front_spec, stats],
        out_specs=(wide, narrow, narrow, pl.BlockSpec((8, HD), lambda k: (0, 0))),
        compiler_params=params(24),
        cost_estimate=cost(5, 384),
    )(length, query, grad, keys, values, front, full)


def add_kernel(num_prompts, owners_ref, terms_ref, _, out_ref):
    count = terms_ref.shape[0]
    total = out_ref.shape[1]
    rows = total // num_prompts
    row_ids = lax.broadcasted_iota(jnp.int32, (total, count), 0)
    col_ids = lax.broadcasted_iota(jnp.int32, (total, count), 1)
    hit = (owners_ref[...] == row_ids // rows) & (row_ids % rows == col_ids % rows)
    sums = nn_dot(jnp.where(hit, 1.0, 0.0).astype(BF16), terms_ref[...]).astype(BF16)
    out_ref[...] = jnp.broadcast_to(sums[None], out_ref.shape)


def add_by_prompt(owners, terms, after, num_prompts, rows, copies):
    return pl.pallas_call(
        functools.partial(add_kernel, num_prompts),
        out_shape=jax.ShapeDtypeStruct((copies, rows * num_prompts, HD), BF16),
        in_specs=[VMEM, VMEM, VMEM],
        out_specs=VMEM,
        compiler_params=params(4),
    )(owners, terms, after)


def place_kernel(parts_ref, key_hbm, value_hbm, out_ref, sems):
    came = [NEAR_ORDER.index(chip) for chip in CHIP_ORDER]
    _, prompts, own, _ = out_ref.shape
    blocks = parts_ref.shape[0] // (2 * KVH)
    rows = own // blocks
    copies = []
    for side, out_hbm in enumerate((key_hbm, value_hbm)):
        for k in range(KVH):
            first = (k * 2 + side) * blocks
            out_ref[side, :, :, k * HD : (k + 1) * HD] = jnp.concatenate(
                [
                    parts_ref[came[first + w]].astype(F32).reshape(prompts, rows, HD)
                    for w in range(blocks)
                ],
                axis=1,
            )
        copies.append(pltpu.make_async_copy(out_ref.at[side], out_hbm, sems.at[side]))
        copies[-1].start()
    for copy in copies:
        copy.wait()


def place(parts, shape):
    return pl.pallas_call(
        place_kernel,
        out_shape=(jax.ShapeDtypeStruct(shape, F32), jax.ShapeDtypeStruct(shape, F32)),
        in_specs=[VMEM],
        out_specs=(HBM, HBM),
        scratch_shapes=[
            pltpu.VMEM((2,) + shape, F32),
            pltpu.SemaphoreType.DMA((2,)),
        ],
        compiler_params=params(4),
    )(parts)


def exchange(blocks, axes, groups):
    return lax.all_to_all(blocks, axes, 0, 0, axis_index_groups=groups)


def shards(query, resp_keys, resp_values, prompt_keys, prompt_values, out_grad, group, lengths):
    places, chips = lax.axis_size("prompt"), lax.axis_size("chip")
    num_prompts, own, width = prompt_keys.shape
    wanted = pick(group, prompt_keys, prompt_values, places)
    front = exchange(wanted, ("prompt", "chip"), front_groups())
    query, grad, keys, values = query[0], out_grad[0], resp_keys[0], resp_values[0]
    rows = 2 * own * width // (chips * HD)
    stats, owners = own_stats(lengths, query, grad, keys, values, group, rows)
    front_grad, full = front_part(lengths, query, grad, front, stats)
    terms = exchange(
        front_grad.reshape(places * chips, rows, HD), ("prompt", "chip"), [FULL_ORDER]
    )
    query_grad, key_grad, value_grad, done = rest_part(
        lengths, query, grad, keys, values, front, full
    )
    terms = lax.all_gather(terms, "core", axis=0).reshape(-1, HD)
    sums = add_by_prompt(owners, terms, done, num_prompts, rows, chips)
    parts = exchange(sums, "chip", [NEAR_ORDER])
    prompt_key_grad, prompt_value_grad = place(parts, prompt_keys.shape)
    return (
        query_grad[None],
        key_grad[None],
        value_grad[None],
        prompt_key_grad,
        prompt_value_grad,
    )


def solution(mesh):
    places, resps = mesh.devices.shape
    mesh = Mesh(
        mesh.devices.reshape(places, resps // CORES, CORES), ("prompt", "chip", "core")
    )
    every = ("prompt", "chip", "core")
    row = P(every, None, None)
    front = P(None, "prompt", None)
    return jax.shard_map(
        shards,
        mesh=mesh,
        in_specs=(row, row, row, front, front, row, P(), P(every)),
        out_specs=(row, row, row, front, front),
        check_vma=False,
    )
```
